512 devices in a mesh: blk: 32 (over x_lo, z, core), group: 16 (over x_hi, y).
Axes of the slice: x: 4 (x_hi: 2, x_lo: 2; x = x_hi * 2 + x_lo), y: 8, z: 8, core: 2. Of those that a mesh axis runs over, the one named last changes fastest.
Arguments:
- pooled_activations: bfloat16 [16, 4096, 1408], P('group', 'blk'), may hold values from -6 to 6
- caption_encodings: bfloat16 [16, 4096, 1152], P('group', 'blk'), may hold values from -6 to 6
- norm_multiplier: float32 [1408], replicated, may hold values from 0.1 to 1.9
- output_projector: bfloat16 [1408, 1152], replicated, may hold values from -0.15625 to 0.15625
- inverse_softness: float32 [1], replicated, may hold values from 30 to 120
- offset_shift: float32 [1], replicated, may hold values from -7 to -4
Outputs:
- loss: float32 [], replicated
- d_features: bfloat16 [16, 4096, 1408], P('group', 'blk')
- d_gain: float32 [1408], replicated
- head_weight_gradient: float32 [1408, 1152], P('blk')
The draws below stay inside these ranges and needn't reach their ends.
All inputs are finite; a program needn't handle non-finite values.
Results may differ from the reference program's by a relative error of at most 0.029.
Values may be sent and summed in bfloat16 or wider, within the bound.
No kernel may reach another device: no remote copies, remote signals or barrier semaphores. Data moves between devices by JAX's collectives and lax.ppermute only.
A program may use at most 64 MiB of HBM per device.

```python
import math
import jax
import jax.numpy as jnp
from jax import lax

W = 1408
E = 1152
PAIR_DEV = 128
PAIRS = 4096
GROUPS = 16
N_BLK = 32


def block_scale(stream_key, shape, cuts, least, largest):
    def one(position, shards_of):
        steps = jax.random.uniform(jax.random.fold_in(jax.random.fold_in(stream_key, 6), position), (shards_of,), jnp.float32, least / len(cuts), largest / len(cuts))
        return jnp.repeat(jnp.exp(steps), shape[position] // shards_of).reshape((-1,) + (1,) * (len(shape) - position - 1))

    factor_of = one(*cuts[0])
    for cut in cuts[1:]:
        factor_of = factor_of * one(*cut)
    return factor_of


def noise(stream_key, dims, width, limit, split=(), dtype=jnp.bfloat16):
    level = block_scale(stream_key, dims, split, -0.22, 0.18) if split else 1.0
    values = jax.random.normal(stream_key, dims, jnp.float32) * width * level
    return jnp.minimum(jnp.maximum(values, -limit), limit).astype(dtype)


def setup_inputs(seed: int = 0) -> dict:
    key_list = jax.random.split(jax.random.key(seed), 7)
    return {
        "pooled_activations": noise(key_list[0], (GROUPS, PAIRS, W), 1.0, 6.0, ((0, 16), (1, 32))),
        "caption_encodings": noise(key_list[1], (GROUPS, PAIRS, E), 1.0, 6.0, ((0, 16), (1, 32))),
        "norm_multiplier": jnp.clip(1.0 + 0.18 * jax.random.normal(key_list[2], (W,), jnp.float32), 0.1, 1.9),
        "output_projector": noise(key_list[3], (W, E), W ** -0.5, 0.15625),
        "inverse_softness": jnp.clip(jnp.exp(jax.random.uniform(key_list[4], (1,), jnp.float32, math.log(30.0), math.log(120.0))), 30.0, 120.0),
        "offset_shift": jnp.clip(jax.random.uniform(key_list[5], (1,), jnp.float32, -7.0, -4.0), -7.0, -4.0),
    }


EPSILON = 1e-06

def reference(pooled_activations, caption_encodings, norm_multiplier, output_projector, inverse_softness, offset_shift):
    similarity_multiplier = inverse_softness[0]
    bias_value = offset_shift[0]

    def one_group(operands):
        feat_rows, text_rows = operands
        values = feat_rows.astype(jnp.float32)
        row_mean = lax.optimization_barrier(jnp.mean(values, axis=1, keepdims=True))
        centred = values - row_mean
        scale_inv = lax.rsqrt(lax.optimization_barrier(jnp.mean(centred * centred, axis=1, keepdims=True)) + EPSILON)
        x_hat = centred * scale_inv
        normed = (x_hat * norm_multiplier).astype(jnp.bfloat16)
        proj = jnp.dot(normed, output_projector, preferred_element_type=jnp.float32)
        pnorm = lax.rsqrt(lax.optimization_barrier(jnp.sum(proj * proj, axis=1, keepdims=True)) + EPSILON)
        unit_img = proj * pnorm
        image_vectors = unit_img.astype(jnp.bfloat16)
        text_vals = text_rows.astype(jnp.float32)
        text_unit = (text_vals * lax.rsqrt(lax.optimization_barrier(jnp.sum(text_vals * text_vals, axis=1, keepdims=True)) + EPSILON)).astype(jnp.bfloat16)
        sims = jnp.dot(image_vectors, text_unit.T, preferred_element_type=jnp.float32)
        pair_logits = similarity_multiplier * sims + bias_value
        row_index = lax.broadcasted_iota(jnp.int32, pair_logits.shape, 0)
        col_index = lax.broadcasted_iota(jnp.int32, pair_logits.shape, 1)
        sign = jnp.where(row_index == col_index, 1.0, -1.0).astype(jnp.float32)
        loss_sum = -jnp.sum(jax.nn.log_sigmoid(sign * pair_logits))
        slope = (-sign * jax.nn.sigmoid(-sign * pair_logits)).astype(jnp.bfloat16)
        image_grad = similarity_multiplier * jnp.dot(slope, text_unit, preferred_element_type=jnp.float32)
        inner = lax.optimization_barrier(jnp.sum(unit_img * image_grad, axis=1, keepdims=True))
        d_proj = ((image_grad - unit_img * inner) * pnorm).astype(jnp.bfloat16)
        d_normed = jnp.dot(d_proj, output_projector.T, preferred_element_type=jnp.float32)
        gain_part = lax.optimization_barrier(jnp.sum(x_hat * d_normed, axis=0))
        d_hat = d_normed * norm_multiplier
        d_feat = scale_inv * (d_hat - lax.optimization_barrier(jnp.mean(d_hat, axis=1, keepdims=True)) - x_hat * lax.optimization_barrier(jnp.mean(d_hat * x_hat, axis=1, keepdims=True)))
        normed_blocks = normed.reshape(N_BLK, PAIR_DEV, W).astype(jnp.float32)
        proj_blocks = d_proj.reshape(N_BLK, PAIR_DEV, E).astype(jnp.float32)
        partial_terms = jnp.einsum('bpw,bpe->bwe', normed_blocks, proj_blocks)
        partial_terms = lax.optimization_barrier(partial_terms.astype(jnp.bfloat16)).astype(jnp.float32)
        return (loss_sum, d_feat.astype(jnp.bfloat16), gain_part, lax.optimization_barrier(jnp.sum(partial_terms, axis=0)))
    loss_entries, d_features, gain_parts, head_parts = lax.map(one_group, (pooled_activations, caption_encodings))
    loss = jnp.sum(loss_entries) / (GROUPS * PAIRS)
    return (loss, d_features, lax.optimization_barrier(jnp.sum(gain_parts, axis=0)), lax.optimization_barrier(jnp.sum(head_parts, axis=0)))
```

```python
import functools

import jax
import jax.numpy as jnp
from jax import lax
from jax.experimental import pallas as pl
from jax.experimental.pallas import tpu as pltpu
from jax.sharding import Mesh, PartitionSpec as P

EPSILON = 1e-06
ROWS = 128
W = 1408
E = 1152
SHARE = 44
F32 = jnp.float32
BF16 = jnp.bfloat16

X, Z, C, HX, Y = "x", "z", "c", "hx", "y"
NZ = 8
N_GROUP = 16
PIECE = 512
BLOCK = 128
EXTRA = 16
GAIN_AT = 112

SWAP = [(0, 1), (1, 0)]
HOP = [
    (z * 2 + c, ((z + (1 if c == 0 else -1)) % NZ) * 2 + c) for z in range(NZ) for c in range(2)
]

VMEM = pl.BlockSpec(memory_space=pltpu.VMEM)
SMEM = pl.BlockSpec(memory_space=pltpu.SMEM)


def call(kernel, out_shape, *operands, specs=None, scratch=(), flops=0, name=None):
    leaves = jax.tree.leaves(out_shape)
    moved = sum(o.size * o.dtype.itemsize for o in (*operands, *leaves))
    return pl.pallas_call(
        kernel,
        out_shape=out_shape,
        in_specs=specs or [VMEM] * len(operands),
        out_specs=jax.tree.map(lambda _: VMEM, out_shape),
        scratch_shapes=list(scratch),
        name=name,
        cost_estimate=pl.CostEstimate(flops=flops, bytes_accessed=moved, transcendentals=0),
        compiler_params=pltpu.CompilerParams(vmem_limit_bytes=48 << 20),
    )(*operands)


def out(shape, dtype):
    return jax.ShapeDtypeStruct(shape, dtype)


def text_kernel(cap_ref, unit_ref):
    values = cap_ref[...].astype(F32)
    scale = lax.rsqrt(jnp.sum(values * values, axis=1, keepdims=True) + EPSILON)
    unit_ref[...] = (values * scale).astype(BF16)


def moments(values):
    mean = jnp.mean(values, axis=1, keepdims=True)
    centred = values - mean
    scale = lax.rsqrt(jnp.mean(centred * centred, axis=1, keepdims=True) + EPSILON)
    return centred * scale, scale


def norm_kernel(x_ref, gain_ref, normed_ref):
    x_hat, _ = moments(x_ref[...].astype(F32))
    normed_ref[...] = (x_hat * gain_ref[...]).astype(BF16)


def project_kernel(where_ref, n0, n1, n2, n3, w_ref, img_ref, unit_ref, pnorm_ref, pick_ref):
    for i, n in enumerate((n0, n2, n1, n3)):
        rows = pl.ds(i * ROWS, ROWS)
        proj = jnp.dot(n[...], w_ref[...], preferred_element_type=F32)
        pnorm = lax.rsqrt(jnp.sum(proj * proj, axis=1, keepdims=True) + EPSILON)
        unit = proj * pnorm
        img_ref[rows, :] = unit.astype(BF16)
        if i < 2:
            unit_ref[rows, :] = unit
            pnorm_ref[rows, :] = jnp.broadcast_to(pnorm, (ROWS, 128))
    row = lax.broadcasted_iota(jnp.int32, (NZ * 48, 1), 0)
    block = row // 48
    inside = row - block * 48
    source = jnp.where(inside < SHARE, SHARE * (where_ref[0] + 2 * block) + inside, -1)
    column = lax.broadcasted_iota(jnp.int32, (NZ * 48, W), 1)
    select = (column == source).astype(F32).astype(BF16)
    for i, n in enumerate((n0, n2, n1, n3)):
        picked = lax.dot_general(
            select, n[...], (((1,), (1,)), ((), ())), preferred_element_type=F32
        )
        pick_ref[:, pl.ds(i * ROWS, ROWS)] = picked.astype(BF16)


def fold_product(grown):
    rows = grown.shape[0]
    while rows > 8:
        rows //= 2
        one, two = grown[:rows], grown[rows:]
        grown = one + two + one * two
    return grown


def fold_sum(values):
    rows = values.shape[0]
    while rows > 8:
        rows //= 2
        values = values[:rows] + values[rows:]
    return values


def log1p(value):
    up = 1.0 + value
    gap = up - 1.0
    return jnp.where(gap == 0.0, value, jnp.log(up) * (value / jnp.where(gap == 0.0, 1.0, gap)))


def pairs_kernel(sc_ref, img_ref, *refs):
    texts, (keep_ref, send_ref, loss_ref, text, slope) = refs[:8], refs[8:]
    for i, piece in enumerate(texts):
        text[pl.ds(i * ROWS, ROWS), :] = piece[...]
    scale, bias = sc_ref[0], sc_ref[1]
    total = jnp.zeros((8, 128), F32)
    span = 256
    for j in range(8 * ROWS // span):
        sims = lax.dot_general(
            img_ref[...],
            text[pl.ds(j * span, span), :],
            (((1,), (1,)), ((), ())),
            preferred_element_type=F32,
        )
        for half in range(span // ROWS):
            chunk = j * (span // ROWS) + half
            turned = scale * sims[:, half * ROWS : (half + 1) * ROWS] + bias
            if chunk == 0:
                shape = (4 * ROWS, ROWS)
                match = lax.broadcasted_iota(jnp.int32, shape, 0) == lax.broadcasted_iota(
                    jnp.int32, shape, 1
                )
                turned = jnp.where(match, -turned, turned)
            small = jnp.exp(-jnp.abs(turned))
            below = 1.0 + small
            inverse = pl.reciprocal(below, approx=True)
            inverse = inverse * (2.0 - below * inverse)
            sig = jnp.where(turned >= 0.0, 1.0, small) * inverse
            if chunk == 0:
                sig = jnp.where(match, -sig, sig)
            slope[:, chunk * ROWS : (chunk + 1) * ROWS] = sig.astype(BF16)
            total = total + fold_sum(jnp.maximum(turned, 0.0)) + log1p(fold_product(small))
    loss = jnp.broadcast_to(jnp.sum(total, keepdims=True), (1, 128))
    loss_ref[...] = loss
    send_ref[2 * ROWS :, :] = loss_rows(loss)
    grad = jnp.dot(slope[...], text[...], preferred_element_type=F32)
    keep_ref[...] = grad[: 2 * ROWS]
    send_ref[: 2 * ROWS, :] = grad[2 * ROWS :].astype(BF16)


def loss_rows(loss):
    high = loss.astype(BF16).astype(F32)
    row = jnp.concatenate([high, loss - high, jnp.zeros((1, E - 256), F32)], axis=1)
    return jnp.broadcast_to(row, (EXTRA, E)).astype(BF16)


def got_loss(got_ref):
    row = got_ref[2 * ROWS :, :256].astype(F32)[:1]
    return row[:, :128] + row[:, 128:]


def add_kernel(keep_ref, loss_ref, got_ref, sum_ref, loss_out, send_ref):
    total = keep_ref[...] + got_ref[: 2 * ROWS, :].astype(F32)
    sum_ref[...] = total
    send_ref[: 2 * ROWS, :] = total.astype(BF16)
    loss = loss_ref[...] + got_loss(got_ref)
    loss_out[...] = loss
    send_ref[2 * ROWS :, :] = loss_rows(loss)


def dproj_kernel(sc_ref, sum_ref, loss_ref, got_ref, unit_ref, pnorm_ref, dproj_ref, loss_out):
    loss_out[...] = loss_ref[...] + got_loss(got_ref)
    for i in range(2):
        rows, other = pl.ds(i * ROWS, ROWS), pl.ds((1 - i) * ROWS, ROWS)
        grad = sc_ref[0] * (sum_ref[rows, :] + got_ref[other, :].astype(F32))
        unit = unit_ref[rows, :]
        inner = jnp.sum(unit * grad, axis=1, keepdims=True)
        dproj_ref[rows, :] = ((grad - unit * inner) * pnorm_ref[rows, 0:1]).astype(BF16)


def back(dproj, w_ref):
    return lax.dot_general(dproj, w_ref[...], (((1,), (1,)), ((), ())), preferred_element_type=F32)


def features_kernel(dproj_ref, x_ref, gain_ref, n0, n2, w_ref, feat_ref, part_ref):
    d_normed = back(dproj_ref[...], w_ref)
    own = d_normed[:ROWS]
    part_ref[...] = jnp.sum(n0[...].astype(F32) * own, axis=0, keepdims=True) + jnp.sum(
        n2[...].astype(F32) * d_normed[ROWS:], axis=0, keepdims=True
    )
    x_hat, scale = moments(x_ref[...].astype(F32))
    d_hat = own * gain_ref[...]
    feat = scale * (
        d_hat
        - jnp.mean(d_hat, axis=1, keepdims=True)
        - x_hat * jnp.mean(d_hat * x_hat, axis=1, keepdims=True)
    )
    feat_ref[...] = feat.astype(BF16)


def head_kernel(own_ref, got_ref, pick_ref, n1, n3, w_ref, gain_ref, part_ref, loss_ref, out_ref):
    head = jnp.dot(pick_ref[:, : 2 * ROWS], own_ref[...], preferred_element_type=F32) + jnp.dot(
        pick_ref[:, 2 * ROWS :], got_ref[...], preferred_element_type=F32
    )
    head = head.astype(BF16)
    d_normed = back(got_ref[...], w_ref)
    gain = part_ref[...] + jnp.sum(n1[...].astype(F32) * d_normed[:ROWS], axis=0, keepdims=True)
    gain = gain + jnp.sum(n3[...].astype(F32) * d_normed[ROWS:], axis=0, keepdims=True)
    gain = gain / gain_ref[...]
    loss = loss_ref[...]
    rows = [gain[:, :512], gain[:, 512:1024], jnp.concatenate([gain[:, 1024:], loss], axis=1)]
    high = [r.astype(BF16).astype(F32) for r in rows]
    low = [r - h for r, h in zip(rows, high)]
    index = lax.broadcasted_iota(jnp.int32, (16, PIECE), 0)
    packed = jnp.zeros((16, PIECE), F32)
    for i, r in enumerate(high + low):
        packed = jnp.where(index == i, r, packed)
    packed = packed.astype(BF16)
    for k in range(NZ):
        block = head[48 * k : 48 * (k + 1)]
        at = BLOCK * k
        out_ref[at : at + 48, :] = block[:, :512]
        out_ref[at + 48 : at + 96, :] = block[:, 512:1024]
        for i in range(3):
            out_ref[at + 96 : at + 112, 128 * i : 128 * (i + 1)] = block[16 * i : 16 * (i + 1), 1024:]
        out_ref[at + 96 : at + 112, 384:] = jnp.zeros((16, 128), BF16)
        out_ref[at + GAIN_AT : at + BLOCK, :] = packed


def reduce_kernel(where_ref, got_ref, out_ref):
    total = got_ref[...].astype(F32).reshape(N_GROUP * NZ, 8, PIECE).sum(axis=0)
    rest = jnp.concatenate([total[3:], total[:3]], axis=0)
    index = lax.broadcasted_iota(jnp.int32, (8, PIECE), 0)
    whole = total + rest
    high = whole.astype(BF16).astype(F32)
    low = whole - high
    moved = jnp.concatenate([low[5:], low[:5]], axis=0)
    split = jnp.where(index < 3, high, jnp.where(index < 6, moved, 0.0))
    piece = jnp.where(where_ref[1] == GAIN_AT // 8, split, total)
    copies = jnp.broadcast_to(piece[None], (N_GROUP, 8, PIECE)).reshape(BLOCK, PIECE)
    out_ref[...] = copies.astype(BF16)


def unpack_kernel(got_ref, head_ref, gain_ref, loss_ref):
    block = got_ref[...].astype(F32)
    head_ref[:, :512] = block[:SHARE]
    head_ref[:, 512:1024] = block[48 : 48 + SHARE]
    tail = block[96:112]
    head_ref[0:16, 1024:] = tail[:, 0:128]
    head_ref[16:32, 1024:] = tail[:, 128:256]
    head_ref[32:SHARE, 1024:] = tail[: SHARE - 32, 256:384]
    rows = block[GAIN_AT : GAIN_AT + 3] + block[GAIN_AT + 3 : GAIN_AT + 6]
    gain_ref[:, :512] = rows[0:1]
    gain_ref[:, 512:1024] = rows[1:2]
    gain_ref[:, 1024:] = rows[2:3, :384]
    loss_ref[...] = rows[2:3, 384:] * (1.0 / (N_GROUP * NZ * 4 * ROWS))


def per_device(pooled, captions, gain, w, scale, bias):
    x = pooled[0]
    gain = gain.reshape(1, W)
    scalars = jnp.concatenate([scale, bias])
    where = jnp.stack(
        [
            lax.axis_index(X) * 16 + lax.axis_index(C),
            lax.axis_index(HX) * 8 + lax.axis_index(Y),
        ]
    ).astype(jnp.int32)

    across = functools.partial(lax.ppermute, axis_name=X, perm=SWAP)
    between = functools.partial(lax.ppermute, axis_name=C, perm=SWAP)
    hop = functools.partial(lax.ppermute, axis_name=(Z, C), perm=HOP)

    text = call(text_kernel, out((ROWS, E), BF16), captions[0], name="text_unit")
    texts = [text]
    one, two = text, between(text)
    for step in range(4):
        one = hop(one)
        texts.append(one)
        if step < 3:
            two = hop(two)
            texts.append(two)

    n0 = call(norm_kernel, out((ROWS, W), BF16), x, gain, name="normed")
    n2 = across(n0)
    n1 = between(n0)
    n3 = between(n2)
    img, unit, pnorm, pick = call(
        project_kernel,
        (
            out((4 * ROWS, E), BF16),
            out((2 * ROWS, E), F32),
            out((2 * ROWS, 128), F32),
            out((NZ * 48, 4 * ROWS), BF16),
        ),
        where,
        n0,
        n1,
        n2,
        n3,
        w,
        specs=[SMEM] + [VMEM] * 5,
        flops=2 * 4 * ROWS * W * (E + NZ * 48),
        name="project",
    )
    keep, send, loss = call(
        pairs_kernel,
        (out((2 * ROWS, E), F32), out((2 * ROWS + EXTRA, E), BF16), out((1, 128), F32)),
        scalars,
        img,
        *texts,
        specs=[SMEM] + [VMEM] * 9,
        scratch=[pltpu.VMEM((8 * ROWS, E), BF16), pltpu.VMEM((4 * ROWS, 8 * ROWS), BF16)],
        flops=4 * 4 * ROWS * 8 * ROWS * E,
        name="pairs",
    )
    total, loss, send = call(
        add_kernel,
        (out((2 * ROWS, E), F32), out((1, 128), F32), out((2 * ROWS + EXTRA, E), BF16)),
        keep,
        loss,
        between(send),
        name="add_cores",
    )
    dproj, loss = call(
        dproj_kernel,
        (out((2 * ROWS, E), BF16), out((1, 128), F32)),
        scalars,
        total,
        loss,
        across(send),
        unit,
        pnorm,
        specs=[SMEM] + [VMEM] * 5,
        name="d_proj",
    )
    dproj_far = between(dproj)
    d_features, gain_part = call(
        features_kernel,
        (out((ROWS, W), BF16), out((1, W), F32)),
        dproj,
        x,
        gain,
        n0,
        n2,
        w,
        flops=4 * ROWS * W * E,
        name="d_features",
    )
    packed = call(
        head_kernel,
        out((NZ * BLOCK, PIECE), BF16),
        dproj,
        dproj_far,
        pick,
        n1,
        n3,
        w,
        gain,
        gain_part,
        loss,
        flops=4 * ROWS * W * E + 8 * ROWS * NZ * 48 * E,
        name="head",
    )
    packed = lax.all_to_all(packed, (Z, HX, Y), 0, 0, tiled=True)
    piece = call(
        reduce_kernel,
        out((BLOCK, PIECE), BF16),
        where,
        packed,
        specs=[SMEM, VMEM],
        name="reduce",
    )
    block = lax.all_to_all(piece, (HX, Y), 0, 0, tiled=True)
    head, d_gain, loss = call(
        unpack_kernel,
        (out((SHARE, E), F32), out((1, W), F32), out((1, 128), F32)),
        block,
        name="unpack",
    )
    return loss[0, 0], d_features[None], d_gain.reshape(W), head


def solution(mesh):
    fine = Mesh(mesh.devices.reshape(2, NZ, 2, 2, 8), (X, Z, C, HX, Y))
    rows = P((HX, Y), (X, Z, C), None)
    return jax.shard_map(
        per_device,
        mesh=fine,
        in_specs=(rows, rows, P(), P(), P(), P()),
        out_specs=(P(), rows, P(), P((X, Z, C), None)),
        check_vma=False,
    )
```

```python
import functools

import jax
import jax.numpy as jnp
from jax import lax
from jax.experimental import pallas as pl
from jax.experimental.pallas import tpu as pltpu
from jax.sharding import Mesh, PartitionSpec as P

EPSILON = 1e-06
ROWS = 128
W = 1408
E = 1152
SHARE = 44
F32 = jnp.float32
BF16 = jnp.bfloat16

X, Z, C, HX, Y = "x", "z", "c", "hx", "y"
NZ = 8
N_GROUP = 16
EARLY, LATE = 5, 3
PIECE = 512
BLOCK = 128
EXTRA = 16
GAIN_AT = 112

SWAP = [(0, 1), (1, 0)]
HOP = [
    (z * 2 + c, ((z + (1 if c == 0 else -1)) % NZ) * 2 + c) for z in range(NZ) for c in range(2)
]

VMEM = pl.BlockSpec(memory_space=pltpu.VMEM)
ANY = pl.BlockSpec(memory_space=pl.ANY)
SMEM = pl.BlockSpec(memory_space=pltpu.SMEM)


def call(kernel, out_shape, *operands, specs=None, outs=None, scratch=(), flops=0, name=None):
    leaves = jax.tree.leaves(out_shape)
    moved = sum(o.size * o.dtype.itemsize for o in (*operands, *leaves))
    return pl.pallas_call(
        kernel,
        out_shape=out_shape,
        in_specs=specs or [VMEM] * len(operands),
        out_specs=outs or jax.tree.map(lambda _: VMEM, out_shape),
        scratch_shapes=list(scratch),
        name=name,
        cost_estimate=pl.CostEstimate(flops=flops, bytes_accessed=moved, transcendentals=0),
        compiler_params=pltpu.CompilerParams(vmem_limit_bytes=32 << 20),
    )(*operands)


def out(shape, dtype):
    return jax.ShapeDtypeStruct(shape, dtype)


def text_kernel(cap_ref, unit_ref):
    values = cap_ref[...].astype(F32)
    scale = lax.rsqrt(jnp.sum(values * values, axis=1, keepdims=True) + EPSILON)
    unit_ref[...] = (values * scale).astype(BF16)


def moments(values):
    mean = jnp.mean(values, axis=1, keepdims=True)
    centred = values - mean
    scale = lax.rsqrt(jnp.mean(centred * centred, axis=1, keepdims=True) + EPSILON)
    return centred * scale, scale


def norm_kernel(x_ref, gain_ref, after_ref, normed_ref):
    del after_ref
    x_hat, _ = moments(x_ref[...].astype(F32))
    normed_ref[...] = (x_hat * gain_ref[...]).astype(BF16)


def project_kernel(n_own, n_far, w_ref, img_ref, unit_ref, pnorm_ref, rows_ref):
    rows_ref[: 2 * ROWS, :] = n_own[...]
    rows_ref[2 * ROWS :, :] = n_far[...]
    proj = jnp.dot(rows_ref[...], w_ref[...], preferred_element_type=F32)
    pnorm = lax.rsqrt(jnp.sum(proj * proj, axis=1, keepdims=True) + EPSILON)
    unit = proj * pnorm
    img_ref[...] = unit.astype(BF16)
    unit_ref[...] = unit[: 2 * ROWS]
    pnorm_ref[...] = jnp.broadcast_to(pnorm[: 2 * ROWS], (2 * ROWS, 128))


def pick_kernel(where_ref, after_ref, n_own, n_far, pick_ref):
    del after_ref
    row = lax.broadcasted_iota(jnp.int32, (NZ * 48, 1), 0)
    block = row // 48
    inside = row - block * 48
    source = jnp.where(inside < SHARE, SHARE * (where_ref[0] + 2 * block) + inside, -1)
    column = lax.broadcasted_iota(jnp.int32, (NZ * 48, W), 1)
    select = (column == source).astype(F32).astype(BF16)
    for i, n in enumerate((n_own, n_far)):
        picked = lax.dot_general(
            select, n[...], (((1,), (1,)), ((), ())), preferred_element_type=F32
        )
        pick_ref[:, 2 * ROWS * i : 2 * ROWS * (i + 1)] = picked.astype(BF16)


def fold_product(grown):
    rows = grown.shape[0]
    while rows > 8:
        rows //= 2
        one, two = grown[:rows], grown[rows:]
        grown = one + two + one * two
    return grown


def fold_sum(values):
    rows = values.shape[0]
    while rows > 8:
        rows //= 2
        values = values[:rows] + values[rows:]
    return values


def log1p(value):
    up = 1.0 + value
    gap = up - 1.0
    return jnp.where(gap == 0.0, value, jnp.log(up) * (value / jnp.where(gap == 0.0, 1.0, gap)))


def pair_terms(sc_ref, img_ref, texts, text, slope, own_first):
    for i, piece in enumerate(texts):
        text[pl.ds(i * ROWS, ROWS), :] = piece[...]
    scale, bias = sc_ref[0], sc_ref[1]
    total = jnp.zeros((8, 128), F32)
    count = len(texts)
    for start in range(0, count, 2):
        span = min(2, count - start)
        sims = lax.dot_general(
            img_ref[...],
            text[pl.ds(start * ROWS, span * ROWS), :],
            (((1,), (1,)), ((), ())),
            preferred_element_type=F32,
        )
        for half in range(span):
            chunk = start + half
            turned = scale * sims[:, half * ROWS : (half + 1) * ROWS] + bias
            if own_first and chunk == 0:
                shape = (4 * ROWS, ROWS)
                match = lax.broadcasted_iota(jnp.int32, shape, 0) == lax.broadcasted_iota(
                    jnp.int32, shape, 1
                )
                turned = jnp.where(match, -turned, turned)
            small = jnp.exp(-jnp.abs(turned))
            below = 1.0 + small
            inverse = pl.reciprocal(below, approx=True)
            inverse = inverse * (2.0 - below * inverse)
            sig = jnp.where(turned >= 0.0, 1.0, small) * inverse
            if own_first and chunk == 0:
                sig = jnp.where(match, -sig, sig)
            slope[:, chunk * ROWS : (chunk + 1) * ROWS] = sig.astype(BF16)
            total = total + fold_sum(jnp.maximum(turned, 0.0)) + log1p(fold_product(small))
    return total


def first_pairs_kernel(sc_ref, img_ref, *refs):
    texts, (grad_ref, loss_ref, text, slope) = refs[:EARLY], refs[EARLY:]
    loss_ref[...] = pair_terms(sc_ref, img_ref, texts, text, slope, True)
    grad_ref[...] = jnp.dot(slope[...], text[...], preferred_element_type=F32)


def last_pairs_kernel(sc_ref, img_ref, grad_ref, part_ref, *refs):
    texts, (keep_ref, send_ref, loss_ref, text, slope) = refs[:LATE], refs[LATE:]
    total = part_ref[...] + pair_terms(sc_ref, img_ref, texts, text, slope, False)
    loss = jnp.broadcast_to(jnp.sum(total, keepdims=True), (1, 128))
    loss_ref[...] = loss
    grad = grad_ref[...] + jnp.dot(slope[...], text[...], preferred_element_type=F32)
    keep_ref[...] = grad[: 2 * ROWS]
    send_ref[: 2 * ROWS, :] = grad[2 * ROWS :].astype(BF16)
    send_ref[2 * ROWS :, :] = loss_rows(loss)


def loss_rows(loss):
    high = loss.astype(BF16).astype(F32)
    row = jnp.concatenate([high, loss - high, jnp.zeros((1, E - 256), F32)], axis=1)
    return jnp.broadcast_to(row, (EXTRA, E)).astype(BF16)


def got_loss(got_ref):
    row = got_ref[2 * ROWS :, :256].astype(F32)[:1]
    return row[:, :128] + row[:, 128:]


def add_kernel(keep_ref, loss_ref, got_ref, sum_ref, loss_out, send_ref):
    total = keep_ref[...] + got_ref[: 2 * ROWS, :].astype(F32)
    sum_ref[...] = total
    send_ref[: 2 * ROWS, :] = total.astype(BF16)
    loss = loss_ref[...] + got_loss(got_ref)
    loss_out[...] = loss
    send_ref[2 * ROWS :, :] = loss_rows(loss)


def dproj_kernel(
    sc_ref, sum_ref, loss_ref, got_ref, unit_ref, pnorm_ref, after_ref, dproj_ref, loss_out
):
    del after_ref
    loss_out[...] = loss_ref[...] + got_loss(got_ref)
    for i in range(2):
        rows, other = pl.ds(i * ROWS, ROWS), pl.ds((1 - i) * ROWS, ROWS)
        grad = sc_ref[0] * (sum_ref[rows, :] + got_ref[other, :].astype(F32))
        unit = unit_ref[rows, :]
        inner = jnp.sum(unit * grad, axis=1, keepdims=True)
        dproj_ref[rows, :] = ((grad - unit * inner) * pnorm_ref[rows, 0:1]).astype(BF16)


def back(dproj, w_ref):
    return lax.dot_general(dproj, w_ref[...], (((1,), (1,)), ((), ())), preferred_element_type=F32)


def features_kernel(dproj_ref, x_ref, gain_ref, n_own, w_ref, feat_ref, part_ref):
    d_normed = back(dproj_ref[...], w_ref)
    own = d_normed[:ROWS]
    part_ref[...] = jnp.sum(n_own[...].astype(F32) * d_normed, axis=0, keepdims=True)
    x_hat, scale = moments(x_ref[...].astype(F32))
    d_hat = own * gain_ref[...]
    feat = scale * (
        d_hat
        - jnp.mean(d_hat, axis=1, keepdims=True)
        - x_hat * jnp.mean(d_hat * x_hat, axis=1, keepdims=True)
    )
    feat_ref[...] = feat.astype(BF16)


def head_kernel(own_ref, got_ref, pick_ref, n_far, w_ref, gain_ref, part_ref, loss_ref, out_ref):
    head = jnp.dot(pick_ref[:, : 2 * ROWS], own_ref[...], preferred_element_type=F32) + jnp.dot(
        pick_ref[:, 2 * ROWS :], got_ref[...], preferred_element_type=F32
    )
    d_normed = back(got_ref[...], w_ref)
    gain = part_ref[...] + jnp.sum(n_far[...].astype(F32) * d_normed, axis=0, keepdims=True)
    gain = gain / gain_ref[...]
    rows = [
        gain[:, :E],
        jnp.concatenate([gain[:, E:], loss_ref[...], jnp.zeros((1, 2 * E - W - 128), F32)], axis=1),
    ]
    high = [r.astype(BF16).astype(F32) for r in rows]
    low = [r - h for r, h in zip(rows, high)]
    index = lax.broadcasted_iota(jnp.int32, (16, E), 0)
    extra = jnp.zeros((16, E), F32)
    for i, r in enumerate(high + low):
        extra = jnp.where(index == 12 + i, r, extra)
    for k in range(NZ):
        out_ref[48 * k : 48 * k + 32, :] = head[48 * k : 48 * k + 32].astype(BF16)
        tail = jnp.where(index < 12, head[48 * k + 32 : 48 * k + 48], extra)
        out_ref[48 * k + 32 : 48 * k + 48, :] = tail.astype(BF16)


def sum_z_kernel(got_ref, out_ref):
    total = got_ref[...].astype(F32).reshape(NZ, 48, E).sum(axis=0)
    out_ref[0:48, :] = total[:, :512].astype(BF16)
    out_ref[48:96, :] = total[:, 512:1024].astype(BF16)
    for i in range(3):
        out_ref[96:112, 128 * i : 128 * (i + 1)] = total[16 * i : 16 * (i + 1), 1024:].astype(BF16)
    out_ref[96:112, 384:] = jnp.zeros((16, 128), BF16)
    both = total[44:46] + total[46:48]
    gain = jnp.concatenate([both[0:1], both[1:2]], axis=1)
    out_ref[GAIN_AT:BLOCK, :] = split_rows(gain[:, :W], gain[:, W : W + 128])


def split_rows(gain, loss):
    rows = [gain[:, :512], gain[:, 512:1024], jnp.concatenate([gain[:, 1024:], loss], axis=1)]
    high = [r.astype(BF16).astype(F32) for r in rows]
    low = [r - h for r, h in zip(rows, high)]
    index = lax.broadcasted_iota(jnp.int32, (16, PIECE), 0)
    packed = jnp.zeros((16, PIECE), F32)
    for i, r in enumerate(high + low):
        packed = jnp.where(index == i, r, packed)
    return packed.astype(BF16)


def sum_groups_kernel(where_ref, got_ref, out_ref):
    total = got_ref[...].astype(F32).reshape(N_GROUP, 8, PIECE).sum(axis=0)
    rest = jnp.concatenate([total[3:], total[:3]], axis=0)
    index = lax.broadcasted_iota(jnp.int32, (8, PIECE), 0)
    whole = total + rest
    high = whole.astype(BF16).astype(F32)
    low = whole - high
    moved = jnp.concatenate([low[5:], low[:5]], axis=0)
    split = jnp.where(index < 3, high, jnp.where(index < 6, moved, 0.0))
    piece = jnp.where(where_ref[1] == GAIN_AT // 8, split, total)
    copies = jnp.broadcast_to(piece[None], (N_GROUP, 8, PIECE)).reshape(BLOCK, PIECE)
    out_ref[...] = copies.astype(BF16)


def unpack_kernel(got_ref, head_ref, gain_ref, loss_ref):
    block = got_ref[...].astype(F32)
    head_ref[:, :512] = block[:SHARE]
    head_ref[:, 512:1024] = block[48 : 48 + SHARE]
    tail = block[96:112]
    head_ref[0:16, 1024:] = tail[:, 0:128]
    head_ref[16:32, 1024:] = tail[:, 128:256]
    head_ref[32:SHARE, 1024:] = tail[: SHARE - 32, 256:384]
    rows = block[GAIN_AT : GAIN_AT + 3] + block[GAIN_AT + 3 : GAIN_AT + 6]
    gain_ref[:, :512] = rows[0:1]
    gain_ref[:, 512:1024] = rows[1:2]
    gain_ref[:, 1024:] = rows[2:3, :384]
    loss_ref[0, 0] = jnp.max(rows[2:3, 384:]) * (1.0 / (N_GROUP * NZ * 4 * ROWS))


def per_device(pooled, captions, gain, w, scale, bias):
    x = pooled[0]
    gain = gain.reshape(1, W)
    scalars = jnp.concatenate([scale, bias])
    where = jnp.stack(
        [
            lax.axis_index(X) * 16 + lax.axis_index(C),
            lax.axis_index(HX) * 8 + lax.axis_index(Y),
        ]
    ).astype(jnp.int32)

    across = functools.partial(lax.ppermute, axis_name=X, perm=SWAP)
    between = functools.partial(lax.ppermute, axis_name=C, perm=SWAP)
    hop = functools.partial(lax.ppermute, axis_name=(Z, C), perm=HOP)

    text = call(text_kernel, out((ROWS, E), BF16), captions[0], name="text_unit")
    texts = [text]
    swapped = between(text)
    one, two = text, swapped
    for step in range(4):
        one = hop(one)
        texts.append(one)
        if step < 3:
            two = hop(two)
            texts.append(two)

    n0 = call(norm_kernel, out((ROWS, W), BF16), x, gain, swapped, specs=[VMEM, VMEM, ANY], name="normed")
    n_own = jnp.concatenate([n0, across(n0)], axis=0)
    n_far = between(n_own)
    img, unit, pnorm = call(
        project_kernel,
        (out((4 * ROWS, E), BF16), out((2 * ROWS, E), F32), out((2 * ROWS, 128), F32)),
        n_own,
        n_far,
        w,
        scratch=[pltpu.VMEM((4 * ROWS, W), BF16)],
        flops=2 * 4 * ROWS * W * E,
        name="project",
    )
    grad, loss = call(
        first_pairs_kernel,
        (out((4 * ROWS, E), F32), out((8, 128), F32)),
        scalars,
        img,
        *texts[:EARLY],
        specs=[SMEM] + [VMEM] * (1 + EARLY),
        scratch=[pltpu.VMEM((EARLY * ROWS, E), BF16), pltpu.VMEM((4 * ROWS, EARLY * ROWS), BF16)],
        flops=4 * 4 * ROWS * EARLY * ROWS * E,
        name="first_pairs",
    )
    keep, send, loss = call(
        last_pairs_kernel,
        (out((2 * ROWS, E), F32), out((2 * ROWS + EXTRA, E), BF16), out((1, 128), F32)),
        scalars,
        img,
        grad,
        loss,
        *texts[EARLY:],
        specs=[SMEM] + [VMEM] * (3 + LATE),
        scratch=[pltpu.VMEM((LATE * ROWS, E), BF16), pltpu.VMEM((4 * ROWS, LATE * ROWS), BF16)],
        flops=4 * 4 * ROWS * LATE * ROWS * E,
        name="last_pairs",
    )
    total, loss, send = call(
        add_kernel,
        (out((2 * ROWS, E), F32), out((1, 128), F32), out((2 * ROWS + EXTRA, E), BF16)),
        keep,
        loss,
        between(send),
        name="add_cores",
    )
    pick = call(
        pick_kernel,
        out((NZ * 48, 4 * ROWS), BF16),
        where,
        loss,
        n_own,
        n_far,
        specs=[SMEM, ANY] + [VMEM] * 2,
        flops=2 * 4 * ROWS * W * NZ * 48,
        name="pick",
    )
    dproj, loss = call(
        dproj_kernel,
        (out((2 * ROWS, E), BF16), out((1, 128), F32)),
        scalars,
        total,
        loss,
        across(send),
        unit,
        pnorm,
        pick,
        specs=[SMEM] + [VMEM] * 5 + [ANY],
        name="d_proj",
    )
    dproj_far = between(dproj)
    d_features, gain_part = call(
        features_kernel,
        (out((ROWS, W), BF16), out((1, W), F32)),
        dproj,
        x,
        gain,
        n_own,
        w,
        flops=4 * ROWS * W * E,
        name="d_features",
    )
    packed = call(
        head_kernel,
        out((NZ * 48, E), BF16),
        dproj,
        dproj_far,
        pick,
        n_far,
        w,
        gain,
        gain_part,
        loss,
        flops=4 * ROWS * W * E + 8 * ROWS * NZ * 48 * E,
        name="head",
    )
    packed = lax.all_to_all(packed, Z, 0, 0, tiled=True)
    block = call(sum_z_kernel, out((BLOCK, PIECE), BF16), packed, name="sum_z")
    block = lax.all_to_all(block, (HX, Y), 0, 0, tiled=True)
    piece = call(
        sum_groups_kernel,
        out((BLOCK, PIECE), BF16),
        where,
        block,
        specs=[SMEM, VMEM],
        name="sum_groups",
    )
    block = lax.all_to_all(piece, (HX, Y), 0, 0, tiled=True)
    head, d_gain, loss = call(
        unpack_kernel,
        (out((SHARE, E), F32), out((1, W), F32), out((1, 1), F32)),
        block,
        outs=(VMEM, VMEM, SMEM),
        name="unpack",
    )
    return loss.reshape(()), d_features[None], d_gain.reshape(W), head


def solution(mesh):
    fine = Mesh(mesh.devices.reshape(2, NZ, 2, 2, 8), (X, Z, C, HX, Y))
    rows = P((HX, Y), (X, Z, C), None)
    return jax.shard_map(
        per_device,
        mesh=fine,
        in_specs=(rows, rows, P(), P(), P(), P()),
        out_specs=(P(), rows, P(), P((X, Z, C), None)),
        check_vma=False,
    )
```

```python
import functools

import jax
import jax.numpy as jnp
from jax import lax
from jax.experimental import pallas as pl
from jax.experimental.pallas import tpu as pltpu
from jax.sharding import Mesh, PartitionSpec as P

EPSILON = 1e-06
ROWS = 128
W = 1408
E = 1152
SHARE = 44
F32 = jnp.float32
BF16 = jnp.bfloat16

X, Z, C, HX, Y = "x", "z", "c", "hx", "y"
NZ = 8
N_GROUP = 16
PIECE = 512
BLOCK = 128
EXTRA = 16
GAIN_AT = 112

SWAP = [(0, 1), (1, 0)]
HOP = [
    (z * 2 + c, ((z + (1 if c == 0 else -1)) % NZ) * 2 + c) for z in range(NZ) for c in range(2)
]

VMEM = pl.BlockSpec(memory_space=pltpu.VMEM)
SMEM = pl.BlockSpec(memory_space=pltpu.SMEM)


def call(kernel, out_shape, *operands, specs=None, outs=None, scratch=(), flops=0, mib=48, name=None):
    leaves = jax.tree.leaves(out_shape)
    moved = sum(o.size * o.dtype.itemsize for o in (*operands, *leaves))
    return pl.pallas_call(
        kernel,
        out_shape=out_shape,
        in_specs=specs or [VMEM] * len(operands),
        out_specs=outs or jax.tree.map(lambda _: VMEM, out_shape),
        scratch_shapes=list(scratch),
        name=name,
        cost_estimate=pl.CostEstimate(flops=flops, bytes_accessed=moved, transcendentals=0),
        compiler_params=pltpu.CompilerParams(vmem_limit_bytes=mib << 20),
    )(*operands)


def out(shape, dtype):
    return jax.ShapeDtypeStruct(shape, dtype)


def moments(values):
    mean = jnp.mean(values, axis=1, keepdims=True)
    centred = values - mean
    scale = lax.rsqrt(jnp.mean(centred * centred, axis=1, keepdims=True) + EPSILON)
    return centred * scale, scale


def prepare_kernel(cap_ref, x_ref, gain_ref, text_ref, both_ref):
    values = cap_ref[...].astype(F32)
    scale = lax.rsqrt(jnp.sum(values * values, axis=1, keepdims=True) + EPSILON)
    text = (values * scale).astype(BF16)
    text_ref[...] = text
    both_ref[:, :E] = text
    x_hat, _ = moments(x_ref[...].astype(F32))
    both_ref[:, E:] = (x_hat * gain_ref[...].reshape(1, W)).astype(BF16)


def unpack_swap_kernel(own_ref, got_ref, text_ref, normed_ref):
    text_ref[...] = got_ref[:, :E]
    normed_ref[:ROWS, :] = own_ref[:, E:]
    normed_ref[ROWS:, :] = got_ref[:, E:]


def collect_kernel(*refs):
    for i, piece in enumerate(refs[:-1]):
        refs[-1][pl.ds(i * ROWS, ROWS), :] = piece[...]


def project_kernel(n_here, n_there, w_ref, after_ref, img_ref, unit_ref, pnorm_ref, rows_ref):
    del after_ref
    for i, part in enumerate((n_here, n_there)):
        rows_ref[i * ROWS : (i + 1) * ROWS, :] = part[:ROWS, :]
        rows_ref[(i + 2) * ROWS : (i + 3) * ROWS, :] = part[ROWS:, :]
    proj = jnp.dot(rows_ref[...], w_ref[...], preferred_element_type=F32)
    pnorm = lax.rsqrt(jnp.sum(proj * proj, axis=1, keepdims=True) + EPSILON)
    unit = proj * pnorm
    img_ref[...] = unit.astype(BF16)
    unit_ref[...] = unit[: 2 * ROWS]
    pnorm_ref[...] = jnp.broadcast_to(pnorm[: 2 * ROWS], (2 * ROWS, 128))


def pick_kernel(after_ref, rows_ref, pick_ref):
    del after_ref
    row = lax.broadcasted_iota(jnp.int32, (NZ * 48, 1), 0)
    block = row // 48
    inside = row - block * 48
    device = lax.axis_index(X) * 16 + lax.axis_index(C)
    source = jnp.where(inside < SHARE, SHARE * (device + 2 * block) + inside, -1)
    column = lax.broadcasted_iota(jnp.int32, (NZ * 48, W), 1)
    select = (column == source).astype(F32).astype(BF16)
    picked = lax.dot_general(
        select, rows_ref[...], (((1,), (1,)), ((), ())), preferred_element_type=F32
    )
    pick_ref[...] = picked.astype(BF16)


def fold_product(grown):
    rows = grown.shape[0]
    while rows > 8:
        rows //= 2
        one, two = grown[:rows], grown[rows:]
        grown = one + two + one * two
    return grown


def fold_sum(values):
    rows = values.shape[0]
    while rows > 8:
        rows //= 2
        values = values[:rows] + values[rows:]
    return values


def log1p(value):
    up = 1.0 + value
    gap = up - 1.0
    return jnp.where(gap == 0.0, value, jnp.log(up) * (value / jnp.where(gap == 0.0, 1.0, gap)))


def pair_terms(scale_ref, bias_ref, img_ref, texts, text, slope):
    text[: 7 * ROWS, :] = texts[0][...]
    text[7 * ROWS :, :] = texts[1][...]
    scale, bias = scale_ref[0], bias_ref[0]
    total = jnp.zeros((8, 128), F32)
    span = 2
    for start in range(0, 8, span):
        sims = lax.dot_general(
            img_ref[...],
            text[pl.ds(start * ROWS, span * ROWS), :],
            (((1,), (1,)), ((), ())),
            preferred_element_type=F32,
        )
        for half in range(span):
            chunk = start + half
            turned = scale * sims[:, half * ROWS : (half + 1) * ROWS] + bias
            if chunk == 0:
                shape = (4 * ROWS, ROWS)
                match = lax.broadcasted_iota(jnp.int32, shape, 0) == lax.broadcasted_iota(
                    jnp.int32, shape, 1
                )
                turned = jnp.where(match, -turned, turned)
            small = jnp.exp(-jnp.abs(turned))
            below = 1.0 + small
            inverse = pltpu.reciprocal(below, approx=True)
            inverse = inverse * (2.0 - below * inverse)
            sig = jnp.where(turned >= 0.0, 1.0, small) * inverse
            if chunk == 0:
                sig = jnp.where(match, -sig, sig)
            slope[:, chunk * ROWS : (chunk + 1) * ROWS] = sig.astype(BF16)
            total = total + fold_sum(jnp.maximum(turned, 0.0)) + log1p(fold_product(small))
    return total


def pairs_kernel(scale_ref, bias_ref, img_ref, *refs):
    texts, (keep_ref, send_ref, loss_ref, text, slope) = refs[:2], refs[2:]
    total = pair_terms(scale_ref, bias_ref, img_ref, texts, text, slope)
    loss = jnp.broadcast_to(jnp.sum(total, keepdims=True), (1, 128))
    loss_ref[...] = loss
    grad = jnp.dot(slope[...], text[...], preferred_element_type=F32)
    keep_ref[...] = grad[: 2 * ROWS]
    send_ref[: 2 * ROWS, :] = grad[2 * ROWS :].astype(BF16)
    send_ref[2 * ROWS :, :] = loss_rows(loss)


def loss_rows(loss):
    high = loss.astype(BF16).astype(F32)
    row = jnp.concatenate([high, loss - high, jnp.zeros((1, E - 256), F32)], axis=1)
    return jnp.broadcast_to(row, (EXTRA, E)).astype(BF16)


def got_loss(got_ref):
    row = got_ref[2 * ROWS :, :256].astype(F32)[:1]
    return row[:, :128] + row[:, 128:]


def add_kernel(keep_ref, loss_ref, got_ref, send_ref):
    total = keep_ref[...] + got_ref[: 2 * ROWS, :].astype(F32)
    send_ref[: 2 * ROWS, :] = total.astype(BF16)
    loss = loss_ref[...] + got_loss(got_ref)
    send_ref[2 * ROWS :, :] = loss_rows(loss)


def dproj_kernel(
    scale_ref, keep_ref, loss_ref, core_ref, got_ref, unit_ref, pnorm_ref, after_ref, dproj_ref, loss_out
):
    del after_ref
    loss_out[...] = loss_ref[...] + got_loss(core_ref) + got_loss(got_ref)
    for i in range(2):
        rows, other = pl.ds(i * ROWS, ROWS), pl.ds((1 - i) * ROWS, ROWS)
        total = keep_ref[rows, :] + core_ref[rows, :].astype(F32)
        grad = scale_ref[0] * (total + got_ref[other, :].astype(F32))
        unit = unit_ref[rows, :]
        inner = jnp.sum(unit * grad, axis=1, keepdims=True)
        dproj_ref[rows, :] = ((grad - unit * inner) * pnorm_ref[rows, 0:1]).astype(BF16)


def back(dproj, w_ref):
    return lax.dot_general(dproj, w_ref[...], (((1,), (1,)), ((), ())), preferred_element_type=F32)


def features_kernel(dproj_ref, x_ref, gain_ref, rows_ref, w_ref, feat_ref, part_ref):
    d_normed = back(dproj_ref[...], w_ref)
    own = d_normed[:ROWS]
    part_ref[...] = jnp.sum(rows_ref[: 2 * ROWS, :].astype(F32) * d_normed, axis=0, keepdims=True)
    x_hat, scale = moments(x_ref[...].astype(F32))
    d_hat = own * gain_ref[...].reshape(1, W)
    feat = scale * (
        d_hat
        - jnp.mean(d_hat, axis=1, keepdims=True)
        - x_hat * jnp.mean(d_hat * x_hat, axis=1, keepdims=True)
    )
    feat_ref[...] = feat.astype(BF16)


def head_kernel(own_ref, got_ref, pick_ref, rows_ref, w_ref, gain_ref, part_ref, loss_ref, out_ref):
    head = jnp.dot(pick_ref[:, : 2 * ROWS], own_ref[...], preferred_element_type=F32) + jnp.dot(
        pick_ref[:, 2 * ROWS :], got_ref[...], preferred_element_type=F32
    )
    head = head.astype(BF16)
    d_normed = back(got_ref[...], w_ref)
    gain = part_ref[...] + jnp.sum(rows_ref[2 * ROWS :, :].astype(F32) * d_normed, axis=0, keepdims=True)
    packed = split_rows(gain / gain_ref[...].reshape(1, W), loss_ref[...])
    for k in range(NZ):
        block = head[48 * k : 48 * (k + 1)]
        at = BLOCK * k
        out_ref[at : at + 48, :] = block[:, :512]
        out_ref[at + 48 : at + 96, :] = block[:, 512:1024]
        for i in range(3):
            out_ref[at + 96 : at + 112, 128 * i : 128 * (i + 1)] = block[16 * i : 16 * (i + 1), 1024:]
        out_ref[at + 96 : at + 112, 384:] = jnp.zeros((16, 128), BF16)
        out_ref[at + GAIN_AT : at + BLOCK, :] = packed


def split_rows(gain, loss):
    rows = [gain[:, :512], gain[:, 512:1024], jnp.concatenate([gain[:, 1024:], loss], axis=1)]
    high = [r.astype(BF16).astype(F32) for r in rows]
    low = [r - h for r, h in zip(rows, high)]
    index = lax.broadcasted_iota(jnp.int32, (16, PIECE), 0)
    packed = jnp.zeros((16, PIECE), F32)
    for i, r in enumerate(high + low):
        packed = jnp.where(index == i, r, packed)
    return packed.astype(BF16)


def reduce_kernel(got_ref, out_ref):
    total = got_ref[...].astype(F32).reshape(N_GROUP * NZ, 8, PIECE).sum(axis=0)
    rest = jnp.concatenate([total[3:], total[:3]], axis=0)
    index = lax.broadcasted_iota(jnp.int32, (8, PIECE), 0)
    whole = total + rest
    high = whole.astype(BF16).astype(F32)
    low = whole - high
    moved = jnp.concatenate([low[5:], low[:5]], axis=0)
    split = jnp.where(index < 3, high, jnp.where(index < 6, moved, 0.0))
    group = lax.axis_index(HX) * 8 + lax.axis_index(Y)
    piece = jnp.where(group == GAIN_AT // 8, split, total)
    copies = jnp.broadcast_to(piece[None], (N_GROUP, 8, PIECE)).reshape(BLOCK, PIECE)
    out_ref[...] = copies.astype(BF16)


def unpack_kernel(got_ref, head_ref, gain_ref, loss_ref):
    block = got_ref[...].astype(F32)
    head_ref[:, :512] = block[:SHARE]
    head_ref[:, 512:1024] = block[48 : 48 + SHARE]
    tail = block[96:112]
    head_ref[0:16, 1024:] = tail[:, 0:128]
    head_ref[16:32, 1024:] = tail[:, 128:256]
    head_ref[32:SHARE, 1024:] = tail[: SHARE - 32, 256:384]
    rows = block[GAIN_AT : GAIN_AT + 3] + block[GAIN_AT + 3 : GAIN_AT + 6]
    gain_ref[...] = jnp.concatenate([rows[0], rows[1], rows[2, :384]])
    loss_ref[0] = jnp.max(rows[2:3, 384:]) * (1.0 / (N_GROUP * NZ * 4 * ROWS))


def per_device(pooled, captions, gain, w, scale, bias):
    x = pooled[0]
    across = functools.partial(lax.ppermute, axis_name=X, perm=SWAP)
    between = functools.partial(lax.ppermute, axis_name=C, perm=SWAP)
    hop = functools.partial(lax.ppermute, axis_name=(Z, C), perm=HOP)

    text, both = call(
        prepare_kernel,
        (out((ROWS, E), BF16), out((ROWS, E + W), BF16)),
        captions[0],
        x,
        gain,
        name="prepare",
    )
    swapped, n_here = call(
        unpack_swap_kernel,
        (out((ROWS, E), BF16), out((2 * ROWS, W), BF16)),
        both,
        between(both),
        name="unpack_swap",
    )
    texts = [text]
    one, two = text, swapped
    for step in range(4):
        one = hop(one)
        if step == 0:
            one, swapped = lax.optimization_barrier((one, swapped))
        texts.append(one)
        if step < 3:
            two = hop(two)
            texts.append(two)

    img, unit, pnorm, rows = call(
        project_kernel,
        (
            out((4 * ROWS, E), BF16),
            out((2 * ROWS, E), F32),
            out((2 * ROWS, 128), F32),
            out((4 * ROWS, W), BF16),
        ),
        n_here,
        across(n_here),
        w,
        texts[5],
        flops=2 * 4 * ROWS * W * E,
        name="project",
    )
    early = call(
        collect_kernel,
        out((7 * ROWS, E), BF16),
        *texts[:7],
        flops=4 * 4 * ROWS * 7 * ROWS * E,
        name="collect",
    )
    keep, send, loss = call(
        pairs_kernel,
        (out((2 * ROWS, E), F32), out((2 * ROWS + EXTRA, E), BF16), out((1, 128), F32)),
        scale,
        bias,
        img,
        early,
        texts[7],
        specs=[SMEM] * 2 + [VMEM] * 3,
        scratch=[pltpu.VMEM((8 * ROWS, E), BF16), pltpu.VMEM((4 * ROWS, 8 * ROWS), BF16)],
        flops=4 * 4 * ROWS * 8 * ROWS * E,
        name="pairs",
    )
    core = between(send)
    send = call(
        add_kernel,
        out((2 * ROWS + EXTRA, E), BF16),
        keep,
        loss,
        core,
        mib=8,
        name="add_cores",
    )
    pick = call(
        pick_kernel,
        out((NZ * 48, 4 * ROWS), BF16),
        send,
        rows,
        flops=2 * 4 * ROWS * W * NZ * 48,
        mib=12,
        name="pick",
    )
    dproj, loss = call(
        dproj_kernel,
        (out((2 * ROWS, E), BF16), out((1, 128), F32)),
        scale,
        keep,
        loss,
        core,
        across(send),
        unit,
        pnorm,
        pick,
        specs=[SMEM] + [VMEM] * 7,
        mib=8,
        name="d_proj",
    )
    dproj_far = between(dproj)
    d_features, gain_part = call(
        features_kernel,
        (out((ROWS, W), BF16), out((1, W), F32)),
        dproj,
        x,
        gain,
        rows,
        w,
        flops=4 * ROWS * W * E,
        mib=16,
        name="d_features",
    )
    packed = call(
        head_kernel,
        out((NZ * BLOCK, PIECE), BF16),
        dproj,
        dproj_far,
        pick,
        rows,
        w,
        gain,
        gain_part,
        loss,
        flops=4 * ROWS * W * E + 8 * ROWS * NZ * 48 * E,
        mib=24,
        name="head",
    )
    packed = lax.all_to_all(packed, (Z, HX, Y), 0, 0, tiled=True)
    piece = call(
        reduce_kernel,
        out((BLOCK, PIECE), BF16),
        packed,
        name="reduce",
    )
    block = lax.all_to_all(piece, (HX, Y), 0, 0, tiled=True)
    head, d_gain, loss = call(
        unpack_kernel,
        (out((SHARE, E), F32), out((W,), F32), out((1,), F32)),
        block,
        outs=(VMEM, VMEM, SMEM),
        name="unpack",
    )
    return loss.reshape(()), d_features[None], d_gain, head


def solution(mesh):
    fine = Mesh(mesh.devices.reshape(2, NZ, 2, 2, 8), (X, Z, C, HX, Y))
    rows = P((HX, Y), (X, Z, C), None)
    return jax.shard_map(
        per_device,
        mesh=fine,
        in_specs=(rows, rows, P(), P(), P(), P()),
        out_specs=(P(), rows, P(), P((X, Z, C), None)),
        check_vma=False,
    )
```

```python
import functools

import jax
import jax.numpy as jnp
from jax import lax
from jax.experimental import pallas as pl
from jax.experimental.pallas import tpu as pltpu
from jax.sharding import Mesh, PartitionSpec as P

EPSILON = 1e-06
ROWS = 128
W = 1408
E = 1152
SHARE = 44
F32 = jnp.float32
BF16 = jnp.bfloat16

X, Z, C, HX, Y = "x", "z", "c", "hx", "y"
NZ = 8
N_GROUP = 16
PIECE = 512
BLOCK = 128
HALF = BLOCK // 2
EXTRA = 16
GAIN_AT = 112

SWAP = [(0, 1), (1, 0)]
HOP = [
    (z * 2 + c, ((z + (1 if c == 0 else -1)) % NZ) * 2 + c) for z in range(NZ) for c in range(2)
]

VMEM = pl.BlockSpec(memory_space=pltpu.VMEM)
SMEM = pl.BlockSpec(memory_space=pltpu.SMEM)


def call(kernel, out_shape, *operands, specs=None, outs=None, scratch=(), flops=0, mib=48, name=None):
    leaves = jax.tree.leaves(out_shape)
    moved = sum(o.size * o.dtype.itemsize for o in (*operands, *leaves))
    return pl.pallas_call(
        kernel,
        out_shape=out_shape,
        in_specs=specs or [VMEM] * len(operands),
        out_specs=outs or jax.tree.map(lambda _: VMEM, out_shape),
        scratch_shapes=list(scratch),
        name=name,
        cost_estimate=pl.CostEstimate(flops=flops, bytes_accessed=moved, transcendentals=0),
        compiler_params=pltpu.CompilerParams(vmem_limit_bytes=mib << 20),
    )(*operands)


def out(shape, dtype):
    return jax.ShapeDtypeStruct(shape, dtype)


def moments(values):
    mean = jnp.mean(values, axis=1, keepdims=True)
    centred = values - mean
    scale = lax.rsqrt(jnp.mean(centred * centred, axis=1, keepdims=True) + EPSILON)
    return centred * scale, scale


def prepare_kernel(cap_ref, x_ref, gain_ref, text_ref, both_ref):
    values = cap_ref[...].astype(F32)
    scale = lax.rsqrt(jnp.sum(values * values, axis=1, keepdims=True) + EPSILON)
    text = (values * scale).astype(BF16)
    text_ref[...] = text
    both_ref[:, :E] = text
    x_hat, _ = moments(x_ref[...].astype(F32))
    both_ref[:, E:] = (x_hat * gain_ref[...].reshape(1, W)).astype(BF16)


def unpack_swap_kernel(own_ref, got_ref, text_ref, normed_ref):
    text_ref[...] = got_ref[:, :E]
    normed_ref[:ROWS, :] = own_ref[:, E:]
    normed_ref[ROWS:, :] = got_ref[:, E:]


def collect_kernel(*refs):
    for i, piece in enumerate(refs[:-1]):
        refs[-1][pl.ds(i * ROWS, ROWS), :] = piece[...]


def project_kernel(n_here, n_there, w_ref, after_ref, img_ref, unit_ref, pnorm_ref, rows_ref):
    del after_ref
    for i, part in enumerate((n_here, n_there)):
        rows_ref[i * ROWS : (i + 1) * ROWS, :] = part[:ROWS, :]
        rows_ref[(i + 2) * ROWS : (i + 3) * ROWS, :] = part[ROWS:, :]
    proj = jnp.dot(rows_ref[...], w_ref[...], preferred_element_type=F32)
    pnorm = lax.rsqrt(jnp.sum(proj * proj, axis=1, keepdims=True) + EPSILON)
    unit = proj * pnorm
    img_ref[...] = unit.astype(BF16)
    unit_ref[...] = unit[: 2 * ROWS]
    pnorm_ref[...] = jnp.broadcast_to(pnorm[: 2 * ROWS], (2 * ROWS, 128))


def pick_kernel(after_ref, rows_ref, pick_ref):
    del after_ref
    row = lax.broadcasted_iota(jnp.int32, (NZ * 48, 1), 0)
    block = row // 48
    inside = row - block * 48
    device = lax.axis_index(X) * 16 + lax.axis_index(C)
    source = jnp.where(inside < SHARE, SHARE * (device + 2 * block) + inside, -1)
    column = lax.broadcasted_iota(jnp.int32, (NZ * 48, W), 1)
    select = (column == source).astype(F32).astype(BF16)
    picked = lax.dot_general(
        select, rows_ref[...], (((1,), (1,)), ((), ())), preferred_element_type=F32
    )
    pick_ref[...] = picked.astype(BF16)


def fold_product(grown):
    rows = grown.shape[0]
    while rows > 8:
        rows //= 2
        one, two = grown[:rows], grown[rows:]
        grown = one + two + one * two
    return grown


def fold_sum(values):
    rows = values.shape[0]
    while rows > 8:
        rows //= 2
        values = values[:rows] + values[rows:]
    return values


def log1p(value):
    up = 1.0 + value
    gap = up - 1.0
    return jnp.where(gap == 0.0, value, jnp.log(up) * (value / jnp.where(gap == 0.0, 1.0, gap)))


def pair_terms(scale_ref, bias_ref, img_ref, texts, text, slope):
    text[: 7 * ROWS, :] = texts[0][...]
    text[7 * ROWS :, :] = texts[1][...]
    scale, bias = scale_ref[0], bias_ref[0]
    total = jnp.zeros((8, 128), F32)
    span = 2
    for start in range(0, 8, span):
        sims = lax.dot_general(
            img_ref[...],
            text[pl.ds(start * ROWS, span * ROWS), :],
            (((1,), (1,)), ((), ())),
            preferred_element_type=F32,
        )
        for half in range(span):
            chunk = start + half
            turned = scale * sims[:, half * ROWS : (half + 1) * ROWS] + bias
            if chunk == 0:
                shape = (4 * ROWS, ROWS)
                match = lax.broadcasted_iota(jnp.int32, shape, 0) == lax.broadcasted_iota(
                    jnp.int32, shape, 1
                )
                turned = jnp.where(match, -turned, turned)
            small = jnp.exp(-jnp.abs(turned))
            below = 1.0 + small
            inverse = pltpu.reciprocal(below, approx=True)
            inverse = inverse * (2.0 - below * inverse)
            sig = jnp.where(turned >= 0.0, 1.0, small) * inverse
            if chunk == 0:
                sig = jnp.where(match, -sig, sig)
            slope[:, chunk * ROWS : (chunk + 1) * ROWS] = sig.astype(BF16)
            total = total + fold_sum(jnp.maximum(turned, 0.0)) + log1p(fold_product(small))
    return total


def pairs_kernel(scale_ref, bias_ref, img_ref, *refs):
    texts, (keep_ref, send_ref, loss_ref, text, slope) = refs[:2], refs[2:]
    total = pair_terms(scale_ref, bias_ref, img_ref, texts, text, slope)
    loss = jnp.broadcast_to(jnp.sum(total, keepdims=True), (1, 128))
    loss_ref[...] = loss
    grad = jnp.dot(slope[...], text[...], preferred_element_type=F32)
    keep_ref[...] = grad[: 2 * ROWS]
    send_ref[: 2 * ROWS, :] = grad[2 * ROWS :].astype(BF16)
    send_ref[2 * ROWS :, :] = loss_rows(loss)


def loss_rows(loss):
    high = loss.astype(BF16).astype(F32)
    row = jnp.concatenate([high, loss - high, jnp.zeros((1, E - 256), F32)], axis=1)
    return jnp.broadcast_to(row, (EXTRA, E)).astype(BF16)


def got_loss(got_ref):
    row = got_ref[2 * ROWS :, :256].astype(F32)[:1]
    return row[:, :128] + row[:, 128:]


def add_kernel(keep_ref, loss_ref, got_ref, send_ref):
    total = keep_ref[...] + got_ref[: 2 * ROWS, :].astype(F32)
    send_ref[: 2 * ROWS, :] = total.astype(BF16)
    loss = loss_ref[...] + got_loss(got_ref)
    send_ref[2 * ROWS :, :] = loss_rows(loss)


def dproj_kernel(
    scale_ref, keep_ref, loss_ref, core_ref, got_ref, unit_ref, pnorm_ref, after_ref, dproj_ref, loss_out
):
    del after_ref
    loss_out[...] = loss_ref[...] + got_loss(core_ref) + got_loss(got_ref)
    for i in range(2):
        rows, other = pl.ds(i * ROWS, ROWS), pl.ds((1 - i) * ROWS, ROWS)
        total = keep_ref[rows, :] + core_ref[rows, :].astype(F32)
        grad = scale_ref[0] * (total + got_ref[other, :].astype(F32))
        unit = unit_ref[rows, :]
        inner = jnp.sum(unit * grad, axis=1, keepdims=True)
        dproj_ref[rows, :] = ((grad - unit * inner) * pnorm_ref[rows, 0:1]).astype(BF16)


def back(dproj, w_ref):
    return lax.dot_general(dproj, w_ref[...], (((1,), (1,)), ((), ())), preferred_element_type=F32)


def features_kernel(dproj_ref, x_ref, gain_ref, rows_ref, w_ref, feat_ref, part_ref):
    d_normed = back(dproj_ref[...], w_ref)
    own = d_normed[:ROWS]
    part_ref[...] = jnp.sum(rows_ref[: 2 * ROWS, :].astype(F32) * d_normed, axis=0, keepdims=True)
    x_hat, scale = moments(x_ref[...].astype(F32))
    d_hat = own * gain_ref[...].reshape(1, W)
    feat = scale * (
        d_hat
        - jnp.mean(d_hat, axis=1, keepdims=True)
        - x_hat * jnp.mean(d_hat * x_hat, axis=1, keepdims=True)
    )
    feat_ref[...] = feat.astype(BF16)


def head_kernel(own_ref, got_ref, pick_ref, rows_ref, w_ref, gain_ref, part_ref, loss_ref, out_ref):
    head = jnp.dot(pick_ref[:, : 2 * ROWS], own_ref[...], preferred_element_type=F32) + jnp.dot(
        pick_ref[:, 2 * ROWS :], got_ref[...], preferred_element_type=F32
    )
    head = head.astype(BF16)
    d_normed = back(got_ref[...], w_ref)
    gain = part_ref[...] + jnp.sum(rows_ref[2 * ROWS :, :].astype(F32) * d_normed, axis=0, keepdims=True)
    packed = split_rows(gain / gain_ref[...].reshape(1, W), loss_ref[...])
    for k in range(NZ):
        block = head[48 * k : 48 * (k + 1)]
        at = BLOCK * k
        out_ref[at : at + 48, :] = block[:, :512]
        out_ref[at + 48 : at + 96, :] = block[:, 512:1024]
        for i in range(3):
            out_ref[at + 96 : at + 112, 128 * i : 128 * (i + 1)] = block[16 * i : 16 * (i + 1), 1024:]
        out_ref[at + 96 : at + 112, 384:] = jnp.zeros((16, 128), BF16)
        out_ref[at + GAIN_AT : at + BLOCK, :] = packed


def split_rows(gain, loss):
    rows = [gain[:, :512], gain[:, 512:1024], jnp.concatenate([gain[:, 1024:], loss], axis=1)]
    high = [r.astype(BF16).astype(F32) for r in rows]
    low = [r - h for r, h in zip(rows, high)]
    index = lax.broadcasted_iota(jnp.int32, (16, PIECE), 0)
    packed = jnp.zeros((16, PIECE), F32)
    for i, r in enumerate(high + low):
        packed = jnp.where(index == i, r, packed)
    return packed.astype(BF16)


def keep_low(total):
    tail = total[HALF - 16 :]
    whole = tail + jnp.concatenate([tail[3:], tail[:3]], axis=0)
    high = whole.astype(BF16).astype(F32)
    low = whole - high
    moved = jnp.concatenate([low[13:], low[:13]], axis=0)
    index = lax.broadcasted_iota(jnp.int32, (16, PIECE), 0)
    split = jnp.where(index < 3, high, jnp.where(index < 6, moved, 0.0))
    split = jnp.where(lax.axis_index(HX) == 1, split, tail)
    return jnp.concatenate([total[: HALF - 16], split], axis=0).astype(BF16)


def sum_near_kernel(got_ref, out_ref):
    total = got_ref[...].astype(F32).reshape(2 * NZ, HALF, PIECE).sum(axis=0)
    half = keep_low(total)
    for i in range(8):
        out_ref[HALF * i : HALF * (i + 1), :] = half


def sum_y_kernel(got_ref, out_ref):
    out_ref[...] = keep_low(got_ref[...].astype(F32).reshape(8, HALF, PIECE).sum(axis=0))


def unpack_kernel(own_ref, other_ref, head_ref, gain_ref, loss_ref):
    first = lax.axis_index(HX) == 0
    own, other = own_ref[...].astype(F32), other_ref[...].astype(F32)
    block = jnp.concatenate([jnp.where(first, own, other), jnp.where(first, other, own)], axis=0)
    head_ref[:, :512] = block[:SHARE]
    head_ref[:, 512:1024] = block[48 : 48 + SHARE]
    tail = block[96:112]
    head_ref[0:16, 1024:] = tail[:, 0:128]
    head_ref[16:32, 1024:] = tail[:, 128:256]
    head_ref[32:SHARE, 1024:] = tail[: SHARE - 32, 256:384]
    rows = block[GAIN_AT : GAIN_AT + 3] + block[GAIN_AT + 3 : GAIN_AT + 6]
    gain_ref[...] = jnp.concatenate([rows[0], rows[1], rows[2, :384]])
    loss_ref[0] = jnp.max(rows[2:3, 384:]) * (1.0 / (N_GROUP * NZ * 4 * ROWS))


def per_device(pooled, captions, gain, w, scale, bias):
    x = pooled[0]
    across = functools.partial(lax.ppermute, axis_name=X, perm=SWAP)
    between = functools.partial(lax.ppermute, axis_name=C, perm=SWAP)
    hop = functools.partial(lax.ppermute, axis_name=(Z, C), perm=HOP)

    text, both = call(
        prepare_kernel,
        (out((ROWS, E), BF16), out((ROWS, E + W), BF16)),
        captions[0],
        x,
        gain,
        name="prepare",
    )
    swapped, n_here = call(
        unpack_swap_kernel,
        (out((ROWS, E), BF16), out((2 * ROWS, W), BF16)),
        both,
        between(both),
        name="unpack_swap",
    )
    texts = [text]
    one, two = text, swapped
    for step in range(4):
        one = hop(one)
        if step == 0:
            one, swapped = lax.optimization_barrier((one, swapped))
        texts.append(one)
        if step < 3:
            two = hop(two)
            texts.append(two)

    img, unit, pnorm, rows = call(
        project_kernel,
        (
            out((4 * ROWS, E), BF16),
            out((2 * ROWS, E), F32),
            out((2 * ROWS, 128), F32),
            out((4 * ROWS, W), BF16),
        ),
        n_here,
        across(n_here),
        w,
        texts[5],
        flops=2 * 4 * ROWS * W * E,
        name="project",
    )
    early = call(
        collect_kernel,
        out((7 * ROWS, E), BF16),
        *texts[:7],
        flops=4 * 4 * ROWS * 7 * ROWS * E,
        name="collect",
    )
    keep, send, loss = call(
        pairs_kernel,
        (out((2 * ROWS, E), F32), out((2 * ROWS + EXTRA, E), BF16), out((1, 128), F32)),
        scale,
        bias,
        img,
        early,
        texts[7],
        specs=[SMEM] * 2 + [VMEM] * 3,
        scratch=[pltpu.VMEM((8 * ROWS, E), BF16), pltpu.VMEM((4 * ROWS, 8 * ROWS), BF16)],
        flops=4 * 4 * ROWS * 8 * ROWS * E,
        name="pairs",
    )
    core = between(send)
    send = call(
        add_kernel,
        out((2 * ROWS + EXTRA, E), BF16),
        keep,
        loss,
        core,
        mib=8,
        name="add_cores",
    )
    pick = call(
        pick_kernel,
        out((NZ * 48, 4 * ROWS), BF16),
        send,
        rows,
        flops=2 * 4 * ROWS * W * NZ * 48,
        mib=12,
        name="pick",
    )
    dproj, loss = call(
        dproj_kernel,
        (out((2 * ROWS, E), BF16), out((1, 128), F32)),
        scale,
        keep,
        loss,
        core,
        across(send),
        unit,
        pnorm,
        pick,
        specs=[SMEM] + [VMEM] * 7,
        mib=8,
        name="d_proj",
    )
    dproj_far = between(dproj)
    d_features, gain_part = call(
        features_kernel,
        (out((ROWS, W), BF16), out((1, W), F32)),
        dproj,
        x,
        gain,
        rows,
        w,
        flops=4 * ROWS * W * E,
        mib=16,
        name="d_features",
    )
    packed = call(
        head_kernel,
        out((NZ * BLOCK, PIECE), BF16),
        dproj,
        dproj_far,
        pick,
        rows,
        w,
        gain,
        gain_part,
        loss,
        flops=4 * ROWS * W * E + 8 * ROWS * NZ * 48 * E,
        mib=24,
        name="head",
    )
    packed = lax.all_to_all(packed, (Z, HX), 0, 0, tiled=True)
    half = call(sum_near_kernel, out((8 * HALF, PIECE), BF16), packed, name="sum_near")
    half = lax.all_to_all(half, Y, 0, 0, tiled=True)
    half = call(sum_y_kernel, out((HALF, PIECE), BF16), half, name="sum_y")
    head, d_gain, loss = call(
        unpack_kernel,
        (out((SHARE, E), F32), out((W,), F32), out((1,), F32)),
        half,
        lax.ppermute(half, HX, SWAP),
        outs=(VMEM, VMEM, SMEM),
        name="unpack",
    )
    return loss.reshape(()), d_features[None], d_gain, head


def solution(mesh):
    fine = Mesh(mesh.devices.reshape(2, NZ, 2, 2, 8), (X, Z, C, HX, Y))
    rows = P((HX, Y), (X, Z, C), None)
    return jax.shard_map(
        per_device,
        mesh=fine,
        in_specs=(rows, rows, P(), P(), P(), P()),
        out_specs=(P(), rows, P(), P((X, Z, C), None)),
        check_vma=False,
    )
```

```python
import functools

import jax
import jax.numpy as jnp
from jax import lax
from jax.experimental import pallas as pl
from jax.experimental.pallas import tpu as pltpu
from jax.sharding import Mesh, PartitionSpec as P

EPSILON = 1e-06
ROWS = 128
W = 1408
E = 1152
SHARE = 44
F32 = jnp.float32
BF16 = jnp.bfloat16

X, Z, C, HX, Y = "x", "z", "c", "hx", "y"
NZ = 8
N_GROUP = 16
PIECE = 896
BLOCK = 64
EXTRA = 16

SWAP = [(0, 1), (1, 0)]
HOP = [
    (z * 2 + c, ((z + (1 if c == 0 else -1)) % NZ) * 2 + c) for z in range(NZ) for c in range(2)
]

VMEM = pl.BlockSpec(memory_space=pltpu.VMEM)
SMEM = pl.BlockSpec(memory_space=pltpu.SMEM)


def call(kernel, out_shape, *operands, specs=None, outs=None, scratch=(), flops=0, mib=48, name=None):
    leaves = jax.tree.leaves(out_shape)
    moved = sum(o.size * o.dtype.itemsize for o in (*operands, *leaves))
    return pl.pallas_call(
        kernel,
        out_shape=out_shape,
        in_specs=specs or [VMEM] * len(operands),
        out_specs=outs or jax.tree.map(lambda _: VMEM, out_shape),
        scratch_shapes=list(scratch),
        name=name,
        cost_estimate=pl.CostEstimate(flops=flops, bytes_accessed=moved, transcendentals=0),
        compiler_params=pltpu.CompilerParams(vmem_limit_bytes=mib << 20),
    )(*operands)


def out(shape, dtype):
    return jax.ShapeDtypeStruct(shape, dtype)


def moments(values):
    mean = jnp.mean(values, axis=1, keepdims=True)
    centred = values - mean
    scale = lax.rsqrt(jnp.mean(centred * centred, axis=1, keepdims=True) + EPSILON)
    return centred * scale, scale


def prepare_kernel(cap_ref, x_ref, gain_ref, text_ref, both_ref):
    values = cap_ref[...].astype(F32)
    scale = lax.rsqrt(jnp.sum(values * values, axis=1, keepdims=True) + EPSILON)
    text = (values * scale).astype(BF16)
    text_ref[...] = text
    both_ref[:, :E] = text
    x_hat, _ = moments(x_ref[...].astype(F32))
    both_ref[:, E:] = (x_hat * gain_ref[...].reshape(1, W)).astype(BF16)


def unpack_swap_kernel(own_ref, got_ref, text_ref, normed_ref):
    text_ref[...] = got_ref[:, :E]
    normed_ref[:ROWS, :] = own_ref[:, E:]
    normed_ref[ROWS:, :] = got_ref[:, E:]


def collect_kernel(*refs):
    for i, piece in enumerate(refs[:-1]):
        refs[-1][pl.ds(i * ROWS, ROWS), :] = piece[...]


def project_kernel(n_here, n_there, w_ref, after_ref, img_ref, unit_ref, pnorm_ref, rows_ref):
    del after_ref
    for i, part in enumerate((n_here, n_there)):
        rows_ref[i * ROWS : (i + 1) * ROWS, :] = part[:ROWS, :]
        rows_ref[(i + 2) * ROWS : (i + 3) * ROWS, :] = part[ROWS:, :]
    proj = jnp.dot(rows_ref[...], w_ref[...], preferred_element_type=F32)
    pnorm = lax.rsqrt(jnp.sum(proj * proj, axis=1, keepdims=True) + EPSILON)
    unit = proj * pnorm
    img_ref[...] = unit.astype(BF16)
    unit_ref[...] = unit[: 2 * ROWS]
    pnorm_ref[...] = jnp.broadcast_to(pnorm[: 2 * ROWS], (2 * ROWS, 128))


def pick_kernel(after_ref, rows_ref, pick_ref):
    del after_ref
    row = lax.broadcasted_iota(jnp.int32, (NZ * 48, 1), 0)
    block = row // 48
    inside = row - block * 48
    device = lax.axis_index(X) * 16 + lax.axis_index(C)
    source = jnp.where(inside < SHARE, SHARE * (device + 2 * block) + inside, -1)
    column = lax.broadcasted_iota(jnp.int32, (NZ * 48, W), 1)
    select = (column == source).astype(F32).astype(BF16)
    picked = lax.dot_general(
        select, rows_ref[...], (((1,), (1,)), ((), ())), preferred_element_type=F32
    )
    pick_ref[...] = picked.astype(BF16)


def fold_product(grown):
    rows = grown.shape[0]
    while rows > 8:
        rows //= 2
        one, two = grown[:rows], grown[rows:]
        grown = one + two + one * two
    return grown


def fold_sum(values):
    rows = values.shape[0]
    while rows > 8:
        rows //= 2
        values = values[:rows] + values[rows:]
    return values


def log1p(value):
    up = 1.0 + value
    gap = up - 1.0
    return jnp.where(gap == 0.0, value, jnp.log(up) * (value / jnp.where(gap == 0.0, 1.0, gap)))


def pair_terms(scale_ref, bias_ref, img_ref, texts, text, slope):
    text[: 7 * ROWS, :] = texts[0][...]
    text[7 * ROWS :, :] = texts[1][...]
    scale, bias = scale_ref[0], bias_ref[0]
    total = jnp.zeros((8, 128), F32)
    span = 2
    for start in range(0, 8, span):
        sims = lax.dot_general(
            img_ref[...],
            text[pl.ds(start * ROWS, span * ROWS), :],
            (((1,), (1,)), ((), ())),
            preferred_element_type=F32,
        )
        for half in range(span):
            chunk = start + half
            turned = scale * sims[:, half * ROWS : (half + 1) * ROWS] + bias
            if chunk == 0:
                shape = (4 * ROWS, ROWS)
                match = lax.broadcasted_iota(jnp.int32, shape, 0) == lax.broadcasted_iota(
                    jnp.int32, shape, 1
                )
                turned = jnp.where(match, -turned, turned)
            small = jnp.exp(-jnp.abs(turned))
            below = 1.0 + small
            inverse = pltpu.reciprocal(below, approx=True)
            inverse = inverse * (2.0 - below * inverse)
            sig = jnp.where(turned >= 0.0, 1.0, small) * inverse
            if chunk == 0:
                sig = jnp.where(match, -sig, sig)
            slope[:, chunk * ROWS : (chunk + 1) * ROWS] = sig.astype(BF16)
            total = total + fold_sum(jnp.maximum(turned, 0.0)) + log1p(fold_product(small))
    return total


def pairs_kernel(scale_ref, bias_ref, img_ref, *refs):
    texts, (keep_ref, send_ref, loss_ref, text, slope) = refs[:2], refs[2:]
    total = pair_terms(scale_ref, bias_ref, img_ref, texts, text, slope)
    loss = jnp.broadcast_to(jnp.sum(total, keepdims=True), (1, 128))
    loss_ref[...] = loss
    grad = jnp.dot(slope[...], text[...], preferred_element_type=F32)
    keep_ref[...] = grad[: 2 * ROWS]
    send_ref[: 2 * ROWS, :] = grad[2 * ROWS :].astype(BF16)
    send_ref[2 * ROWS :, :] = loss_rows(loss)


def loss_rows(loss):
    high = loss.astype(BF16).astype(F32)
    row = jnp.concatenate([high, loss - high, jnp.zeros((1, E - 256), F32)], axis=1)
    return jnp.broadcast_to(row, (EXTRA, E)).astype(BF16)


def got_loss(got_ref):
    row = got_ref[2 * ROWS :, :256].astype(F32)[:1]
    return row[:, :128] + row[:, 128:]


def add_kernel(keep_ref, loss_ref, got_ref, send_ref):
    total = keep_ref[...] + got_ref[: 2 * ROWS, :].astype(F32)
    send_ref[: 2 * ROWS, :] = total.astype(BF16)
    loss = loss_ref[...] + got_loss(got_ref)
    send_ref[2 * ROWS :, :] = loss_rows(loss)


def dproj_kernel(
    scale_ref, keep_ref, loss_ref, core_ref, got_ref, unit_ref, pnorm_ref, after_ref, dproj_ref, loss_out
):
    del after_ref
    loss_out[...] = loss_ref[...] + got_loss(core_ref) + got_loss(got_ref)
    for i in range(2):
        rows, other = pl.ds(i * ROWS, ROWS), pl.ds((1 - i) * ROWS, ROWS)
        total = keep_ref[rows, :] + core_ref[rows, :].astype(F32)
        grad = scale_ref[0] * (total + got_ref[other, :].astype(F32))
        unit = unit_ref[rows, :]
        inner = jnp.sum(unit * grad, axis=1, keepdims=True)
        dproj_ref[rows, :] = ((grad - unit * inner) * pnorm_ref[rows, 0:1]).astype(BF16)


def back(dproj, w_ref):
    return lax.dot_general(dproj, w_ref[...], (((1,), (1,)), ((), ())), preferred_element_type=F32)


def features_kernel(dproj_ref, x_ref, gain_ref, rows_ref, w_ref, feat_ref, part_ref):
    d_normed = back(dproj_ref[...], w_ref)
    own = d_normed[:ROWS]
    part_ref[...] = jnp.sum(rows_ref[: 2 * ROWS, :].astype(F32) * d_normed, axis=0, keepdims=True)
    x_hat, scale = moments(x_ref[...].astype(F32))
    d_hat = own * gain_ref[...].reshape(1, W)
    feat = scale * (
        d_hat
        - jnp.mean(d_hat, axis=1, keepdims=True)
        - x_hat * jnp.mean(d_hat * x_hat, axis=1, keepdims=True)
    )
    feat_ref[...] = feat.astype(BF16)


def split_rows(first, second):
    high = [r.astype(BF16).astype(F32) for r in (first, second)]
    return high + [first - high[0], second - high[1]]


def head_kernel(own_ref, got_ref, pick_ref, rows_ref, w_ref, gain_ref, part_ref, loss_ref, out_ref):
    head = jnp.dot(pick_ref[:, : 2 * ROWS], own_ref[...], preferred_element_type=F32) + jnp.dot(
        pick_ref[:, 2 * ROWS :], got_ref[...], preferred_element_type=F32
    )
    d_normed = back(got_ref[...], w_ref)
    gain = part_ref[...] + jnp.sum(rows_ref[2 * ROWS :, :].astype(F32) * d_normed, axis=0, keepdims=True)
    gain = gain / gain_ref[...].reshape(1, W)
    rest = [gain[:, PIECE:], loss_ref[...], jnp.zeros((1, 2 * PIECE - W - 128), F32)]
    extra = split_rows(gain[:, :PIECE], jnp.concatenate(rest, axis=1))
    index = lax.broadcasted_iota(jnp.int32, (16, PIECE), 0)
    for k in range(NZ):
        block = head[48 * k : 48 * (k + 1)]
        at = BLOCK * k
        out_ref[at : at + 32, :] = block[:32, :PIECE].astype(BF16)
        tail = block[32:, :PIECE]
        for i, row in enumerate(extra):
            tail = jnp.where(index == 12 + i, row, tail)
        out_ref[at + 32 : at + 48, :] = tail.astype(BF16)
        for i in range(3):
            side = block[16 * i : 16 * (i + 1), PIECE:].astype(BF16)
            out_ref[at + 48 : at + 64, 256 * i : 256 * (i + 1)] = side
        out_ref[at + 48 : at + 64, 768:] = jnp.zeros((16, 128), BF16)


def reduce_kernel(got_ref, out_ref):
    total = got_ref[...].astype(F32).reshape(8 * NZ, 8, PIECE).sum(axis=0)
    index = lax.broadcasted_iota(jnp.int32, (8, PIECE), 0)
    split = total
    for i, row in enumerate(split_rows(total[4:5] + total[6:7], total[5:6] + total[7:8])):
        split = jnp.where(index == 4 + i, row, split)
    piece = jnp.where(lax.axis_index(Y) == 5, split, total)
    copies = jnp.broadcast_to(piece[None], (N_GROUP, 8, PIECE)).reshape(8 * N_GROUP, PIECE)
    out_ref[...] = copies.astype(BF16)


def unpack_kernel(got_ref, head_ref, gain_ref, loss_ref):
    block = got_ref[:BLOCK, :].astype(F32) + got_ref[BLOCK:, :].astype(F32)
    head_ref[:, :PIECE] = block[:SHARE]
    head_ref[0:16, PIECE:] = block[48:64, 0:256]
    head_ref[16:32, PIECE:] = block[48:64, 256:512]
    head_ref[32:SHARE, PIECE:] = block[48 : 48 + SHARE - 32, 512:768]
    rows = block[44:46] + block[46:48]
    gain_ref[...] = jnp.concatenate([rows[0], rows[1, : W - PIECE]])
    loss = rows[1:2, W - PIECE : W - PIECE + 128]
    loss_ref[0] = jnp.max(loss) * (1.0 / (N_GROUP * NZ * 4 * ROWS))


def per_device(pooled, captions, gain, w, scale, bias):
    x = pooled[0]
    across = functools.partial(lax.ppermute, axis_name=X, perm=SWAP)
    between = functools.partial(lax.ppermute, axis_name=C, perm=SWAP)
    hop = functools.partial(lax.ppermute, axis_name=(Z, C), perm=HOP)

    text, both = call(
        prepare_kernel,
        (out((ROWS, E), BF16), out((ROWS, E + W), BF16)),
        captions[0],
        x,
        gain,
        name="prepare",
    )
    swapped, n_here = call(
        unpack_swap_kernel,
        (out((ROWS, E), BF16), out((2 * ROWS, W), BF16)),
        both,
        between(both),
        name="unpack_swap",
    )
    texts = [text]
    one, two = text, swapped
    for step in range(4):
        one = hop(one)
        if step == 0:
            one, swapped = lax.optimization_barrier((one, swapped))
        texts.append(one)
        if step < 3:
            two = hop(two)
            texts.append(two)

    img, unit, pnorm, rows = call(
        project_kernel,
        (
            out((4 * ROWS, E), BF16),
            out((2 * ROWS, E), F32),
            out((2 * ROWS, 128), F32),
            out((4 * ROWS, W), BF16),
        ),
        n_here,
        across(n_here),
        w,
        texts[5],
        flops=2 * 4 * ROWS * W * E,
        name="project",
    )
    early = call(
        collect_kernel,
        out((7 * ROWS, E), BF16),
        *texts[:7],
        flops=4 * 4 * ROWS * 7 * ROWS * E,
        name="collect",
    )
    keep, send, loss = call(
        pairs_kernel,
        (out((2 * ROWS, E), F32), out((2 * ROWS + EXTRA, E), BF16), out((1, 128), F32)),
        scale,
        bias,
        img,
        early,
        texts[7],
        specs=[SMEM] * 2 + [VMEM] * 3,
        scratch=[pltpu.VMEM((8 * ROWS, E), BF16), pltpu.VMEM((4 * ROWS, 8 * ROWS), BF16)],
        flops=4 * 4 * ROWS * 8 * ROWS * E,
        name="pairs",
    )
    core = between(send)
    send = call(
        add_kernel,
        out((2 * ROWS + EXTRA, E), BF16),
        keep,
        loss,
        core,
        mib=8,
        name="add_cores",
    )
    pick = call(
        pick_kernel,
        out((NZ * 48, 4 * ROWS), BF16),
        send,
        rows,
        flops=2 * 4 * ROWS * W * NZ * 48,
        mib=12,
        name="pick",
    )
    dproj, loss = call(
        dproj_kernel,
        (out((2 * ROWS, E), BF16), out((1, 128), F32)),
        scale,
        keep,
        loss,
        core,
        across(send),
        unit,
        pnorm,
        pick,
        specs=[SMEM] + [VMEM] * 7,
        mib=8,
        name="d_proj",
    )
    dproj_far = between(dproj)
    d_features, gain_part = call(
        features_kernel,
        (out((ROWS, W), BF16), out((1, W), F32)),
        dproj,
        x,
        gain,
        rows,
        w,
        flops=4 * ROWS * W * E,
        mib=16,
        name="d_features",
    )
    packed = call(
        head_kernel,
        out((NZ * BLOCK, PIECE), BF16),
        dproj,
        dproj_far,
        pick,
        rows,
        w,
        gain,
        gain_part,
        loss,
        flops=4 * ROWS * W * E + 8 * ROWS * NZ * 48 * E,
        mib=24,
        name="head",
    )
    packed = lax.all_to_all(packed, (Z, Y), 0, 0, tiled=True)
    piece = call(
        reduce_kernel,
        out((8 * N_GROUP, PIECE), BF16),
        packed,
        name="reduce",
    )
    block = lax.all_to_all(piece, (HX, Y), 0, 0, tiled=True)
    head, d_gain, loss = call(
        unpack_kernel,
        (out((SHARE, E), F32), out((W,), F32), out((1,), F32)),
        block,
        outs=(VMEM, VMEM, SMEM),
        name="unpack",
    )
    return loss.reshape(()), d_features[None], d_gain, head


def solution(mesh):
    fine = Mesh(mesh.devices.reshape(2, NZ, 2, 2, 8), (X, Z, C, HX, Y))
    rows = P((HX, Y), (X, Z, C), None)
    return jax.shard_map(
        per_device,
        mesh=fine,
        in_specs=(rows, rows, P(), P(), P(), P()),
        out_specs=(P(), rows, P(), P((X, Z, C), None)),
        check_vma=False,
    )
```

```python
import functools

import jax
import jax.numpy as jnp
from jax import lax
from jax.experimental import pallas as pl
from jax.experimental.pallas import tpu as pltpu
from jax.sharding import Mesh, PartitionSpec as P

EPSILON = 1e-06
ROWS = 128
W = 1408
E = 1152
SHARE = 44
F32 = jnp.float32
BF16 = jnp.bfloat16

X, Z, C, HX, Y = "x", "z", "c", "hx", "y"
NZ = 8
N_GROUP = 16
PIECE = 896
BLOCK = 64
EXTRA = 16

SWAP = [(0, 1), (1, 0)]
HOP = [
    (z * 2 + c, ((z + (1 if c == 0 else -1)) % NZ) * 2 + c) for z in range(NZ) for c in range(2)
]

HOP_BACK = [(there, here) for here, there in HOP]

VMEM = pl.BlockSpec(memory_space=pltpu.VMEM)
SMEM = pl.BlockSpec(memory_space=pltpu.SMEM)


def call(kernel, out_shape, *operands, specs=None, outs=None, scratch=(), flops=0, mib=48, name=None):
    leaves = jax.tree.leaves(out_shape)
    moved = sum(o.size * o.dtype.itemsize for o in (*operands, *leaves))
    return pl.pallas_call(
        kernel,
        out_shape=out_shape,
        in_specs=specs or [VMEM] * len(operands),
        out_specs=outs or jax.tree.map(lambda _: VMEM, out_shape),
        scratch_shapes=list(scratch),
        name=name,
        cost_estimate=pl.CostEstimate(flops=flops, bytes_accessed=moved, transcendentals=0),
        compiler_params=pltpu.CompilerParams(vmem_limit_bytes=mib << 20),
    )(*operands)


def out(shape, dtype):
    return jax.ShapeDtypeStruct(shape, dtype)


def moments(values):
    mean = jnp.mean(values, axis=1, keepdims=True)
    centred = values - mean
    scale = lax.rsqrt(jnp.mean(centred * centred, axis=1, keepdims=True) + EPSILON)
    return centred * scale, scale


def text_kernel(cap_ref, text_ref):
    values = cap_ref[...].astype(F32)
    scale = lax.rsqrt(jnp.sum(values * values, axis=1, keepdims=True) + EPSILON)
    text_ref[...] = (values * scale).astype(BF16)


def norm_kernel(x_ref, gain_ref, normed_ref):
    x_hat, _ = moments(x_ref[...].astype(F32))
    normed_ref[...] = (x_hat * gain_ref[...].reshape(1, W)).astype(BF16)


def join_kernel(own_ref, got_ref, both_ref):
    both_ref[:ROWS, :] = own_ref[...]
    both_ref[ROWS:, :] = got_ref[...]


def collect_kernel(*refs):
    for i, piece in enumerate(refs[:-1]):
        refs[-1][pl.ds(i * ROWS, ROWS), :] = piece[...]


def project_kernel(n_here, n_there, w_ref, after_ref, img_ref, unit_ref, pnorm_ref, rows_ref):
    del after_ref
    for i, part in enumerate((n_here, n_there)):
        rows_ref[i * ROWS : (i + 1) * ROWS, :] = part[:ROWS, :]
        rows_ref[(i + 2) * ROWS : (i + 3) * ROWS, :] = part[ROWS:, :]
    proj = jnp.dot(rows_ref[...], w_ref[...], preferred_element_type=F32)
    pnorm = lax.rsqrt(jnp.sum(proj * proj, axis=1, keepdims=True) + EPSILON)
    unit = proj * pnorm
    img_ref[...] = unit.astype(BF16)
    unit_ref[...] = unit[: 2 * ROWS]
    pnorm_ref[...] = jnp.broadcast_to(pnorm[: 2 * ROWS], (2 * ROWS, 128))


def pick_kernel(after_ref, rows_ref, pick_ref):
    del after_ref
    row = lax.broadcasted_iota(jnp.int32, (NZ * 48, 1), 0)
    block = row // 48
    inside = row - block * 48
    device = lax.axis_index(X) * 16 + lax.axis_index(C)
    source = jnp.where(inside < SHARE, SHARE * (device + 2 * block) + inside, -1)
    column = lax.broadcasted_iota(jnp.int32, (NZ * 48, W), 1)
    select = (column == source).astype(F32).astype(BF16)
    picked = lax.dot_general(
        select, rows_ref[...], (((1,), (1,)), ((), ())), preferred_element_type=F32
    )
    pick_ref[...] = picked.astype(BF16)


def fold_product(grown):
    rows = grown.shape[0]
    while rows > 8:
        rows //= 2
        one, two = grown[:rows], grown[rows:]
        grown = one + two + one * two
    return grown


def fold_sum(values):
    rows = values.shape[0]
    while rows > 8:
        rows //= 2
        values = values[:rows] + values[rows:]
    return values


def log1p(value):
    up = 1.0 + value
    gap = up - 1.0
    return jnp.where(gap == 0.0, value, jnp.log(up) * (value / jnp.where(gap == 0.0, 1.0, gap)))


def pair_terms(scale_ref, bias_ref, img_ref, texts, text, slope):
    text[: 7 * ROWS, :] = texts[0][...]
    text[7 * ROWS :, :] = texts[1][...]
    scale, bias = scale_ref[0], bias_ref[0]
    total = jnp.zeros((8, 128), F32)
    span = 2
    for start in range(0, 8, span):
        sims = lax.dot_general(
            img_ref[...],
            text[pl.ds(start * ROWS, span * ROWS), :],
            (((1,), (1,)), ((), ())),
            preferred_element_type=F32,
        )
        for half in range(span):
            chunk = start + half
            turned = scale * sims[:, half * ROWS : (half + 1) * ROWS] + bias
            if chunk == 0:
                shape = (4 * ROWS, ROWS)
                match = lax.broadcasted_iota(jnp.int32, shape, 0) == lax.broadcasted_iota(
                    jnp.int32, shape, 1
                )
                turned = jnp.where(match, -turned, turned)
            small = jnp.exp(-jnp.abs(turned))
            below = 1.0 + small
            inverse = pltpu.reciprocal(below, approx=True)
            inverse = inverse * (2.0 - below * inverse)
            sig = jnp.where(turned >= 0.0, 1.0, small) * inverse
            if chunk == 0:
                sig = jnp.where(match, -sig, sig)
            slope[:, chunk * ROWS : (chunk + 1) * ROWS] = sig.astype(BF16)
            total = total + fold_sum(jnp.maximum(turned, 0.0)) + log1p(fold_product(small))
    return total


def pairs_kernel(scale_ref, bias_ref, img_ref, *refs):
    texts, (keep_ref, send_ref, loss_ref, text, slope) = refs[:2], refs[2:]
    total = pair_terms(scale_ref, bias_ref, img_ref, texts, text, slope)
    loss = jnp.broadcast_to(jnp.sum(total, keepdims=True), (1, 128))
    loss_ref[...] = loss
    grad = jnp.dot(slope[...], text[...], preferred_element_type=F32)
    keep_ref[...] = grad[: 2 * ROWS]
    send_ref[: 2 * ROWS, :] = grad[2 * ROWS :].astype(BF16)
    send_ref[2 * ROWS :, :] = loss_rows(loss)


def loss_rows(loss):
    high = loss.astype(BF16).astype(F32)
    row = jnp.concatenate([high, loss - high, jnp.zeros((1, E - 256), F32)], axis=1)
    return jnp.broadcast_to(row, (EXTRA, E)).astype(BF16)


def got_loss(got_ref):
    row = got_ref[2 * ROWS :, :256].astype(F32)[:1]
    return row[:, :128] + row[:, 128:]


def add_kernel(keep_ref, loss_ref, got_ref, send_ref):
    total = keep_ref[...] + got_ref[: 2 * ROWS, :].astype(F32)
    send_ref[: 2 * ROWS, :] = total.astype(BF16)
    loss = loss_ref[...] + got_loss(got_ref)
    send_ref[2 * ROWS :, :] = loss_rows(loss)


def dproj_kernel(
    scale_ref, keep_ref, loss_ref, core_ref, got_ref, unit_ref, pnorm_ref, after_ref, dproj_ref, loss_out
):
    del after_ref
    loss_out[...] = loss_ref[...] + got_loss(core_ref) + got_loss(got_ref)
    for i in range(2):
        rows, other = pl.ds(i * ROWS, ROWS), pl.ds((1 - i) * ROWS, ROWS)
        total = keep_ref[rows, :] + core_ref[rows, :].astype(F32)
        grad = scale_ref[0] * (total + got_ref[other, :].astype(F32))
        unit = unit_ref[rows, :]
        inner = jnp.sum(unit * grad, axis=1, keepdims=True)
        dproj_ref[rows, :] = ((grad - unit * inner) * pnorm_ref[rows, 0:1]).astype(BF16)


def back(dproj, w_ref):
    return lax.dot_general(dproj, w_ref[...], (((1,), (1,)), ((), ())), preferred_element_type=F32)


def features_kernel(dproj_ref, x_ref, gain_ref, rows_ref, w_ref, feat_ref, part_ref):
    d_normed = back(dproj_ref[...], w_ref)
    own = d_normed[:ROWS]
    part_ref[...] = jnp.sum(rows_ref[: 2 * ROWS, :].astype(F32) * d_normed, axis=0, keepdims=True)
    x_hat, scale = moments(x_ref[...].astype(F32))
    d_hat = own * gain_ref[...].reshape(1, W)
    feat = scale * (
        d_hat
        - jnp.mean(d_hat, axis=1, keepdims=True)
        - x_hat * jnp.mean(d_hat * x_hat, axis=1, keepdims=True)
    )
    feat_ref[...] = feat.astype(BF16)


def split_rows(first, second):
    high = [r.astype(BF16).astype(F32) for r in (first, second)]
    return high + [first - high[0], second - high[1]]


def head_kernel(own_ref, got_ref, pick_ref, rows_ref, w_ref, gain_ref, part_ref, loss_ref, out_ref):
    head = jnp.dot(pick_ref[:, : 2 * ROWS], own_ref[...], preferred_element_type=F32) + jnp.dot(
        pick_ref[:, 2 * ROWS :], got_ref[...], preferred_element_type=F32
    )
    d_normed = back(got_ref[...], w_ref)
    gain = part_ref[...] + jnp.sum(rows_ref[2 * ROWS :, :].astype(F32) * d_normed, axis=0, keepdims=True)
    gain = gain / gain_ref[...].reshape(1, W)
    rest = [gain[:, PIECE:], loss_ref[...], jnp.zeros((1, 2 * PIECE - W - 128), F32)]
    extra = split_rows(gain[:, :PIECE], jnp.concatenate(rest, axis=1))
    index = lax.broadcasted_iota(jnp.int32, (16, PIECE), 0)
    for k in range(NZ):
        block = head[48 * k : 48 * (k + 1)]
        at = BLOCK * k
        out_ref[at : at + 32, :] = block[:32, :PIECE].astype(BF16)
        tail = block[32:, :PIECE]
        for i, row in enumerate(extra):
            tail = jnp.where(index == 12 + i, row, tail)
        out_ref[at + 32 : at + 48, :] = tail.astype(BF16)
        for i in range(3):
            side = block[16 * i : 16 * (i + 1), PIECE:].astype(BF16)
            out_ref[at + 48 : at + 64, 256 * i : 256 * (i + 1)] = side
        out_ref[at + 48 : at + 64, 768:] = jnp.zeros((16, 128), BF16)


def reduce_kernel(got_ref, out_ref):
    total = got_ref[...].astype(F32).reshape(8 * NZ, 8, PIECE).sum(axis=0)
    index = lax.broadcasted_iota(jnp.int32, (8, PIECE), 0)
    split = total
    for i, row in enumerate(split_rows(total[4:5] + total[6:7], total[5:6] + total[7:8])):
        split = jnp.where(index == 4 + i, row, split)
    piece = jnp.where(lax.axis_index(Y) == 5, split, total)
    copies = jnp.broadcast_to(piece[None], (N_GROUP, 8, PIECE)).reshape(8 * N_GROUP, PIECE)
    out_ref[...] = copies.astype(BF16)


def unpack_kernel(got_ref, head_ref, gain_ref, loss_ref):
    block = got_ref[:BLOCK, :].astype(F32) + got_ref[BLOCK:, :].astype(F32)
    head_ref[:, :PIECE] = block[:SHARE]
    head_ref[0:16, PIECE:] = block[48:64, 0:256]
    head_ref[16:32, PIECE:] = block[48:64, 256:512]
    head_ref[32:SHARE, PIECE:] = block[48 : 48 + SHARE - 32, 512:768]
    rows = block[44:46] + block[46:48]
    gain_ref[...] = jnp.concatenate([rows[0], rows[1, : W - PIECE]])
    loss = rows[1:2, W - PIECE : W - PIECE + 128]
    loss_ref[0] = jnp.max(loss) * (1.0 / (N_GROUP * NZ * 4 * ROWS))


def per_device(pooled, captions, gain, w, scale, bias):
    x = pooled[0]
    across = functools.partial(lax.ppermute, axis_name=X, perm=SWAP)
    between = functools.partial(lax.ppermute, axis_name=C, perm=SWAP)
    hop = functools.partial(lax.ppermute, axis_name=(Z, C), perm=HOP)
    hop_back = functools.partial(lax.ppermute, axis_name=(Z, C), perm=HOP_BACK)

    text = call(text_kernel, out((ROWS, E), BF16), captions[0], name="text_unit")
    texts = [text]
    one, two = text, text
    for step in range(4):
        one = hop(one)
        texts.append(one)
        if step < 3:
            two = hop_back(two)
            texts.append(two)

    n0 = call(norm_kernel, out((ROWS, W), BF16), x, gain, name="normed")
    n_here = call(join_kernel, out((2 * ROWS, W), BF16), n0, between(n0), name="join")
    img, unit, pnorm, rows = call(
        project_kernel,
        (
            out((4 * ROWS, E), BF16),
            out((2 * ROWS, E), F32),
            out((2 * ROWS, 128), F32),
            out((4 * ROWS, W), BF16),
        ),
        n_here,
        across(n_here),
        w,
        texts[5],
        flops=2 * 4 * ROWS * W * E,
        name="project",
    )
    early = call(
        collect_kernel,
        out((7 * ROWS, E), BF16),
        *texts[:7],
        flops=4 * 4 * ROWS * 7 * ROWS * E,
        name="collect",
    )
    keep, send, loss = call(
        pairs_kernel,
        (out((2 * ROWS, E), F32), out((2 * ROWS + EXTRA, E), BF16), out((1, 128), F32)),
        scale,
        bias,
        img,
        early,
        texts[7],
        specs=[SMEM] * 2 + [VMEM] * 3,
        scratch=[pltpu.VMEM((8 * ROWS, E), BF16), pltpu.VMEM((4 * ROWS, 8 * ROWS), BF16)],
        flops=4 * 4 * ROWS * 8 * ROWS * E,
        name="pairs",
    )
    core = between(send)
    send = call(
        add_kernel,
        out((2 * ROWS + EXTRA, E), BF16),
        keep,
        loss,
        core,
        mib=8,
        name="add_cores",
    )
    pick = call(
        pick_kernel,
        out((NZ * 48, 4 * ROWS), BF16),
        send,
        rows,
        flops=2 * 4 * ROWS * W * NZ * 48,
        mib=12,
        name="pick",
    )
    dproj, loss = call(
        dproj_kernel,
        (out((2 * ROWS, E), BF16), out((1, 128), F32)),
        scale,
        keep,
        loss,
        core,
        across(send),
        unit,
        pnorm,
        pick,
        specs=[SMEM] + [VMEM] * 7,
        mib=8,
        name="d_proj",
    )
    dproj_far = between(dproj)
    d_features, gain_part = call(
        features_kernel,
        (out((ROWS, W), BF16), out((1, W), F32)),
        dproj,
        x,
        gain,
        rows,
        w,
        flops=4 * ROWS * W * E,
        mib=16,
        name="d_features",
    )
    packed = call(
        head_kernel,
        out((NZ * BLOCK, PIECE), BF16),
        dproj,
        dproj_far,
        pick,
        rows,
        w,
        gain,
        gain_part,
        loss,
        flops=4 * ROWS * W * E + 8 * ROWS * NZ * 48 * E,
        mib=24,
        name="head",
    )
    packed = lax.all_to_all(packed, (Z, Y), 0, 0, tiled=True)
    piece = call(
        reduce_kernel,
        out((8 * N_GROUP, PIECE), BF16),
        packed,
        name="reduce",
    )
    block = lax.all_to_all(piece, (HX, Y), 0, 0, tiled=True)
    head, d_gain, loss = call(
        unpack_kernel,
        (out((SHARE, E), F32), out((W,), F32), out((1,), F32)),
        block,
        outs=(VMEM, VMEM, SMEM),
        name="unpack",
    )
    return loss.reshape(()), d_features[None], d_gain, head


def solution(mesh):
    fine = Mesh(mesh.devices.reshape(2, NZ, 2, 2, 8), (X, Z, C, HX, Y))
    rows = P((HX, Y), (X, Z, C), None)
    return jax.shard_map(
        per_device,
        mesh=fine,
        in_specs=(rows, rows, P(), P(), P(), P()),
        out_specs=(P(), rows, P(), P((X, Z, C), None)),
        check_vma=False,
    )
```

```python
import functools

import jax
import jax.numpy as jnp
from jax import lax
from jax.experimental import pallas as pl
from jax.experimental.pallas import tpu as pltpu
from jax.sharding import Mesh, PartitionSpec as P

EPSILON = 1e-06
ROWS = 128
W = 1408
E = 1152
SHARE = 44
F32 = jnp.float32
BF16 = jnp.bfloat16

X, Z, C, HX, Y = "x", "z", "c", "hx", "y"
NZ = 8
N_GROUP = 16
PIECE = 896
BLOCK = 64
EXTRA = 16

SWAP = [(0, 1), (1, 0)]
HOP = [
    (z * 2 + c, ((z + (1 if c == 0 else -1)) % NZ) * 2 + c) for z in range(NZ) for c in range(2)
]

VMEM = pl.BlockSpec(memory_space=pltpu.VMEM)
SMEM = pl.BlockSpec(memory_space=pltpu.SMEM)


def call(kernel, out_shape, *operands, specs=None, outs=None, scratch=(), flops=0, mib=48, name=None):
    leaves = jax.tree.leaves(out_shape)
    moved = sum(o.size * o.dtype.itemsize for o in (*operands, *leaves))
    return pl.pallas_call(
        kernel,
        out_shape=out_shape,
        in_specs=specs or [VMEM] * len(operands),
        out_specs=outs or jax.tree.map(lambda _: VMEM, out_shape),
        scratch_shapes=list(scratch),
        name=name,
        cost_estimate=pl.CostEstimate(flops=flops, bytes_accessed=moved, transcendentals=0),
        compiler_params=pltpu.CompilerParams(vmem_limit_bytes=mib << 20),
    )(*operands)


def out(shape, dtype):
    return jax.ShapeDtypeStruct(shape, dtype)


def moments(values):
    mean = jnp.mean(values, axis=1, keepdims=True)
    centred = values - mean
    scale = lax.rsqrt(jnp.mean(centred * centred, axis=1, keepdims=True) + EPSILON)
    return centred * scale, scale


def prepare_kernel(cap_ref, x_ref, gain_ref, text_ref, both_ref):
    values = cap_ref[...].astype(F32)
    scale = lax.rsqrt(jnp.sum(values * values, axis=1, keepdims=True) + EPSILON)
    text = (values * scale).astype(BF16)
    text_ref[...] = text
    both_ref[:, :E] = text
    x_hat, _ = moments(x_ref[...].astype(F32))
    both_ref[:, E:] = (x_hat * gain_ref[...].reshape(1, W)).astype(BF16)


def unpack_swap_kernel(own_ref, got_ref, text_ref, normed_ref):
    text_ref[...] = got_ref[:, :E]
    normed_ref[:ROWS, :] = own_ref[:, E:]
    normed_ref[ROWS:, :] = got_ref[:, E:]


def collect_kernel(*refs):
    for i, piece in enumerate(refs[:-1]):
        refs[-1][pl.ds(i * ROWS, ROWS), :] = piece[...]


def project_kernel(n_here, n_there, w_ref, after_ref, img_ref, unit_ref, pnorm_ref, rows_ref):
    del after_ref
    for i, part in enumerate((n_here, n_there)):
        rows_ref[i * ROWS : (i + 1) * ROWS, :] = part[:ROWS, :]
        rows_ref[(i + 2) * ROWS : (i + 3) * ROWS, :] = part[ROWS:, :]
    proj = jnp.dot(rows_ref[...], w_ref[...], preferred_element_type=F32)
    pnorm = lax.rsqrt(jnp.sum(proj * proj, axis=1, keepdims=True) + EPSILON)
    unit = proj * pnorm
    img_ref[...] = unit.astype(BF16)
    unit_ref[...] = unit[: 2 * ROWS]
    pnorm_ref[...] = jnp.broadcast_to(pnorm[: 2 * ROWS], (2 * ROWS, 128))


def pick_kernel(after_ref, rows_ref, pick_ref):
    del after_ref
    row = lax.broadcasted_iota(jnp.int32, (NZ * 48, 1), 0)
    block = row // 48
    inside = row - block * 48
    device = lax.axis_index(X) * 16 + lax.axis_index(C)
    source = jnp.where(inside < SHARE, SHARE * (device + 2 * block) + inside, -1)
    column = lax.broadcasted_iota(jnp.int32, (NZ * 48, W), 1)
    select = (column == source).astype(F32).astype(BF16)
    picked = lax.dot_general(
        select, rows_ref[...], (((1,), (1,)), ((), ())), preferred_element_type=F32
    )
    pick_ref[...] = picked.astype(BF16)


def fold_product(grown):
    rows = grown.shape[0]
    while rows > 8:
        rows //= 2
        one, two = grown[:rows], grown[rows:]
        grown = one + two + one * two
    return grown


def fold_sum(values):
    rows = values.shape[0]
    while rows > 8:
        rows //= 2
        values = values[:rows] + values[rows:]
    return values


def log1p(value):
    up = 1.0 + value
    gap = up - 1.0
    return jnp.where(gap == 0.0, value, jnp.log(up) * (value / jnp.where(gap == 0.0, 1.0, gap)))


def pair_terms(scale_ref, bias_ref, img_ref, texts, text, slope):
    text[: 7 * ROWS, :] = texts[0][...]
    text[7 * ROWS :, :] = texts[1][...]
    scale, bias = scale_ref[0], bias_ref[0]
    total = jnp.zeros((8, 128), F32)
    span = 2
    for start in range(0, 8, span):
        sims = lax.dot_general(
            img_ref[...],
            text[pl.ds(start * ROWS, span * ROWS), :],
            (((1,), (1,)), ((), ())),
            preferred_element_type=F32,
        )
        for half in range(span):
            chunk = start + half
            turned = scale * sims[:, half * ROWS : (half + 1) * ROWS] + bias
            if chunk == 0:
                shape = (4 * ROWS, ROWS)
                match = lax.broadcasted_iota(jnp.int32, shape, 0) == lax.broadcasted_iota(
                    jnp.int32, shape, 1
                )
                turned = jnp.where(match, -turned, turned)
            small = jnp.exp(-jnp.abs(turned))
            below = 1.0 + small
            inverse = pltpu.reciprocal(below, approx=True)
            inverse = inverse * (2.0 - below * inverse)
            sig = jnp.where(turned >= 0.0, 1.0, small) * inverse
            if chunk == 0:
                sig = jnp.where(match, -sig, sig)
            slope[:, chunk * ROWS : (chunk + 1) * ROWS] = sig.astype(BF16)
            total = total + fold_sum(jnp.maximum(turned, 0.0)) + log1p(fold_product(small))
    return total


def pairs_kernel(scale_ref, bias_ref, img_ref, *refs):
    texts, (send_ref, loss_ref, slope, text) = refs[:2], refs[2:]
    total = pair_terms(scale_ref, bias_ref, img_ref, texts, text, slope)
    loss = jnp.broadcast_to(jnp.sum(total, keepdims=True), (1, 128))
    loss_ref[...] = loss
    grad = jnp.dot(slope[2 * ROWS :, :], text[...], preferred_element_type=F32)
    send_ref[: 2 * ROWS, :] = grad.astype(BF16)
    send_ref[2 * ROWS :, :] = loss_rows(loss)


def keep_kernel(slope_ref, early_ref, last_ref, keep_ref):
    early = jnp.dot(slope_ref[: 2 * ROWS, : 7 * ROWS], early_ref[...], preferred_element_type=F32)
    last = jnp.dot(slope_ref[: 2 * ROWS, 7 * ROWS :], last_ref[...], preferred_element_type=F32)
    keep_ref[...] = early + last


def loss_rows(loss):
    high = loss.astype(BF16).astype(F32)
    row = jnp.concatenate([high, loss - high, jnp.zeros((1, E - 256), F32)], axis=1)
    return jnp.broadcast_to(row, (EXTRA, E)).astype(BF16)


def got_loss(got_ref):
    row = got_ref[2 * ROWS :, :256].astype(F32)[:1]
    return row[:, :128] + row[:, 128:]


def add_kernel(keep_ref, loss_ref, got_ref, send_ref):
    total = keep_ref[...] + got_ref[: 2 * ROWS, :].astype(F32)
    send_ref[: 2 * ROWS, :] = total.astype(BF16)
    loss = loss_ref[...] + got_loss(got_ref)
    send_ref[2 * ROWS :, :] = loss_rows(loss)


def dproj_kernel(
    scale_ref, keep_ref, loss_ref, core_ref, got_ref, unit_ref, pnorm_ref, after_ref, dproj_ref, loss_out
):
    del after_ref
    loss_out[...] = loss_ref[...] + got_loss(core_ref) + got_loss(got_ref)
    for i in range(2):
        rows, other = pl.ds(i * ROWS, ROWS), pl.ds((1 - i) * ROWS, ROWS)
        total = keep_ref[rows, :] + core_ref[rows, :].astype(F32)
        grad = scale_ref[0] * (total + got_ref[other, :].astype(F32))
        unit = unit_ref[rows, :]
        inner = jnp.sum(unit * grad, axis=1, keepdims=True)
        dproj_ref[rows, :] = ((grad - unit * inner) * pnorm_ref[rows, 0:1]).astype(BF16)


def back(dproj, w_ref):
    return lax.dot_general(dproj, w_ref[...], (((1,), (1,)), ((), ())), preferred_element_type=F32)


def features_kernel(dproj_ref, x_ref, gain_ref, rows_ref, w_ref, feat_ref, part_ref):
    d_normed = back(dproj_ref[...], w_ref)
    own = d_normed[:ROWS]
    part_ref[...] = jnp.sum(rows_ref[: 2 * ROWS, :].astype(F32) * d_normed, axis=0, keepdims=True)
    x_hat, scale = moments(x_ref[...].astype(F32))
    d_hat = own * gain_ref[...].reshape(1, W)
    feat = scale * (
        d_hat
        - jnp.mean(d_hat, axis=1, keepdims=True)
        - x_hat * jnp.mean(d_hat * x_hat, axis=1, keepdims=True)
    )
    feat_ref[...] = feat.astype(BF16)


def split_rows(first, second):
    high = [r.astype(BF16).astype(F32) for r in (first, second)]
    return high + [first - high[0], second - high[1]]


def head_kernel(own_ref, got_ref, pick_ref, rows_ref, w_ref, gain_ref, part_ref, loss_ref, out_ref):
    head = jnp.dot(pick_ref[:, : 2 * ROWS], own_ref[...], preferred_element_type=F32) + jnp.dot(
        pick_ref[:, 2 * ROWS :], got_ref[...], preferred_element_type=F32
    )
    d_normed = back(got_ref[...], w_ref)
    gain = part_ref[...] + jnp.sum(rows_ref[2 * ROWS :, :].astype(F32) * d_normed, axis=0, keepdims=True)
    gain = gain / gain_ref[...].reshape(1, W)
    rest = [gain[:, PIECE:], loss_ref[...], jnp.zeros((1, 2 * PIECE - W - 128), F32)]
    extra = split_rows(gain[:, :PIECE], jnp.concatenate(rest, axis=1))
    index = lax.broadcasted_iota(jnp.int32, (16, PIECE), 0)
    for k in range(NZ):
        block = head[48 * k : 48 * (k + 1)]
        at = BLOCK * k
        out_ref[at : at + 32, :] = block[:32, :PIECE].astype(BF16)
        tail = block[32:, :PIECE]
        for i, row in enumerate(extra):
            tail = jnp.where(index == 12 + i, row, tail)
        out_ref[at + 32 : at + 48, :] = tail.astype(BF16)
        for i in range(3):
            side = block[16 * i : 16 * (i + 1), PIECE:].astype(BF16)
            out_ref[at + 48 : at + 64, 256 * i : 256 * (i + 1)] = side
        out_ref[at + 48 : at + 64, 768:] = jnp.zeros((16, 128), BF16)


def reduce_kernel(got_ref, out_ref):
    total = got_ref[...].astype(F32).reshape(8 * NZ, 8, PIECE).sum(axis=0)
    index = lax.broadcasted_iota(jnp.int32, (8, PIECE), 0)
    split = total
    for i, row in enumerate(split_rows(total[4:5] + total[6:7], total[5:6] + total[7:8])):
        split = jnp.where(index == 4 + i, row, split)
    piece = jnp.where(lax.axis_index(Y) == 5, split, total)
    copies = jnp.broadcast_to(piece[None], (N_GROUP, 8, PIECE)).reshape(8 * N_GROUP, PIECE)
    out_ref[...] = copies.astype(BF16)


def unpack_kernel(got_ref, head_ref, gain_ref, loss_ref):
    block = got_ref[:BLOCK, :].astype(F32) + got_ref[BLOCK:, :].astype(F32)
    head_ref[:, :PIECE] = block[:SHARE]
    head_ref[0:16, PIECE:] = block[48:64, 0:256]
    head_ref[16:32, PIECE:] = block[48:64, 256:512]
    head_ref[32:SHARE, PIECE:] = block[48 : 48 + SHARE - 32, 512:768]
    rows = block[44:46] + block[46:48]
    gain_ref[...] = jnp.concatenate([rows[0], rows[1, : W - PIECE]])
    loss = rows[1:2, W - PIECE : W - PIECE + 128]
    loss_ref[0] = jnp.max(loss) * (1.0 / (N_GROUP * NZ * 4 * ROWS))


def per_device(pooled, captions, gain, w, scale, bias):
    x = pooled[0]
    across = functools.partial(lax.ppermute, axis_name=X, perm=SWAP)
    between = functools.partial(lax.ppermute, axis_name=C, perm=SWAP)
    hop = functools.partial(lax.ppermute, axis_name=(Z, C), perm=HOP)

    text, both = call(
        prepare_kernel,
        (out((ROWS, E), BF16), out((ROWS, E + W), BF16)),
        captions[0],
        x,
        gain,
        name="prepare",
    )
    swapped, n_here = call(
        unpack_swap_kernel,
        (out((ROWS, E), BF16), out((2 * ROWS, W), BF16)),
        both,
        between(both),
        name="unpack_swap",
    )
    texts = [text]
    one, two = text, swapped
    for step in range(4):
        one = hop(one)
        if step == 0:
            one, swapped = lax.optimization_barrier((one, swapped))
        texts.append(one)
        if step < 3:
            two = hop(two)
            texts.append(two)

    img, unit, pnorm, rows = call(
        project_kernel,
        (
            out((4 * ROWS, E), BF16),
            out((2 * ROWS, E), F32),
            out((2 * ROWS, 128), F32),
            out((4 * ROWS, W), BF16),
        ),
        n_here,
        across(n_here),
        w,
        texts[5],
        flops=2 * 4 * ROWS * W * E,
        name="project",
    )
    early = call(
        collect_kernel,
        out((7 * ROWS, E), BF16),
        *texts[:7],
        flops=4 * 4 * ROWS * 7 * ROWS * E,
        name="collect",
    )
    send, loss, slope = call(
        pairs_kernel,
        (
            out((2 * ROWS + EXTRA, E), BF16),
            out((1, 128), F32),
            out((4 * ROWS, 8 * ROWS), BF16),
        ),
        scale,
        bias,
        img,
        early,
        texts[7],
        specs=[SMEM] * 2 + [VMEM] * 3,
        scratch=[pltpu.VMEM((8 * ROWS, E), BF16)],
        flops=3 * 4 * ROWS * 8 * ROWS * E,
        name="pairs",
    )
    core = between(send)
    keep = call(
        keep_kernel,
        out((2 * ROWS, E), F32),
        slope,
        early,
        texts[7],
        flops=4 * ROWS * 8 * ROWS * E,
        name="keep",
    )
    send = call(
        add_kernel,
        out((2 * ROWS + EXTRA, E), BF16),
        keep,
        loss,
        core,
        mib=8,
        name="add_cores",
    )
    pick = call(
        pick_kernel,
        out((NZ * 48, 4 * ROWS), BF16),
        send,
        rows,
        flops=2 * 4 * ROWS * W * NZ * 48,
        mib=12,
        name="pick",
    )
    dproj, loss = call(
        dproj_kernel,
        (out((2 * ROWS, E), BF16), out((1, 128), F32)),
        scale,
        keep,
        loss,
        core,
        across(send),
        unit,
        pnorm,
        pick,
        specs=[SMEM] + [VMEM] * 7,
        mib=8,
        name="d_proj",
    )
    dproj_far = between(dproj)
    d_features, gain_part = call(
        features_kernel,
        (out((ROWS, W), BF16), out((1, W), F32)),
        dproj,
        x,
        gain,
        rows,
        w,
        flops=4 * ROWS * W * E,
        mib=16,
        name="d_features",
    )
    packed = call(
        head_kernel,
        out((NZ * BLOCK, PIECE), BF16),
        dproj,
        dproj_far,
        pick,
        rows,
        w,
        gain,
        gain_part,
        loss,
        flops=4 * ROWS * W * E + 8 * ROWS * NZ * 48 * E,
        mib=24,
        name="head",
    )
    packed = lax.all_to_all(packed, (Z, Y), 0, 0, tiled=True)
    piece = call(
        reduce_kernel,
        out((8 * N_GROUP, PIECE), BF16),
        packed,
        name="reduce",
    )
    block = lax.all_to_all(piece, (HX, Y), 0, 0, tiled=True)
    head, d_gain, loss = call(
        unpack_kernel,
        (out((SHARE, E), F32), out((W,), F32), out((1,), F32)),
        block,
        outs=(VMEM, VMEM, SMEM),
        name="unpack",
    )
    return loss.reshape(()), d_features[None], d_gain, head


def solution(mesh):
    fine = Mesh(mesh.devices.reshape(2, NZ, 2, 2, 8), (X, Z, C, HX, Y))
    rows = P((HX, Y), (X, Z, C), None)
    return jax.shard_map(
        per_device,
        mesh=fine,
        in_specs=(rows, rows, P(), P(), P(), P()),
        out_specs=(P(), rows, P(), P((X, Z, C), None)),
        check_vma=False,
    )
```

```python
import functools

import jax
import jax.numpy as jnp
from jax import lax
from jax.experimental import pallas as pl
from jax.experimental.pallas import tpu as pltpu
from jax.sharding import Mesh, PartitionSpec as P

EPSILON = 1e-06
ROWS = 128
W = 1408
E = 1152
SHARE = 44
F32 = jnp.float32
BF16 = jnp.bfloat16

X, Z, C, HX, Y = "x", "z", "c", "hx", "y"
NZ = 8
N_GROUP = 16
PIECE = 896
BLOCK = 64
EXTRA = 16

SWAP = [(0, 1), (1, 0)]
HOP = [
    (z * 2 + c, ((z + (1 if c == 0 else -1)) % NZ) * 2 + c) for z in range(NZ) for c in range(2)
]

HOP_BACK = [(there, here) for here, there in HOP]

VMEM = pl.BlockSpec(memory_space=pltpu.VMEM)
SMEM = pl.BlockSpec(memory_space=pltpu.SMEM)


def call(kernel, out_shape, *operands, specs=None, outs=None, scratch=(), flops=0, mib=48, name=None):
    leaves = jax.tree.leaves(out_shape)
    moved = sum(o.size * o.dtype.itemsize for o in (*operands, *leaves))
    return pl.pallas_call(
        kernel,
        out_shape=out_shape,
        in_specs=specs or [VMEM] * len(operands),
        out_specs=outs or jax.tree.map(lambda _: VMEM, out_shape),
        scratch_shapes=list(scratch),
        name=name,
        cost_estimate=pl.CostEstimate(flops=flops, bytes_accessed=moved, transcendentals=0),
        compiler_params=pltpu.CompilerParams(vmem_limit_bytes=mib << 20),
    )(*operands)


def out(shape, dtype):
    return jax.ShapeDtypeStruct(shape, dtype)


def moments(values):
    mean = jnp.mean(values, axis=1, keepdims=True)
    centred = values - mean
    scale = lax.rsqrt(jnp.mean(centred * centred, axis=1, keepdims=True) + EPSILON)
    return centred * scale, scale


def text_kernel(cap_ref, text_ref):
    values = cap_ref[...].astype(F32)
    scale = lax.rsqrt(jnp.sum(values * values, axis=1, keepdims=True) + EPSILON)
    text_ref[...] = (values * scale).astype(BF16)


def norm_kernel(x_ref, gain_ref, normed_ref):
    x_hat, _ = moments(x_ref[...].astype(F32))
    normed_ref[...] = (x_hat * gain_ref[...].reshape(1, W)).astype(BF16)


def join_kernel(own_ref, got_ref, both_ref):
    both_ref[:ROWS, :] = own_ref[...]
    both_ref[ROWS:, :] = got_ref[...]


def collect_kernel(*refs):
    for i, piece in enumerate(refs[:-1]):
        refs[-1][pl.ds(i * ROWS, ROWS), :] = piece[...]


def project_kernel(n_own, n_core, w_ref, after_ref, img_ref, unit_ref, pnorm_ref, rows_ref):
    del after_ref
    rows_ref[: 2 * ROWS, :] = n_own[...]
    rows_ref[2 * ROWS :, :] = n_core[...]
    proj = jnp.dot(rows_ref[...], w_ref[...], preferred_element_type=F32)
    pnorm = lax.rsqrt(jnp.sum(proj * proj, axis=1, keepdims=True) + EPSILON)
    unit = proj * pnorm
    img_ref[...] = unit.astype(BF16)
    unit_ref[...] = unit[: 2 * ROWS]
    pnorm_ref[...] = jnp.broadcast_to(pnorm[: 2 * ROWS], (2 * ROWS, 128))


def pick_kernel(after_ref, rows_ref, pick_ref):
    del after_ref
    row = lax.broadcasted_iota(jnp.int32, (NZ * 48, 1), 0)
    block = row // 48
    inside = row - block * 48
    device = lax.axis_index(X) * 16 + lax.axis_index(C)
    source = jnp.where(inside < SHARE, SHARE * (device + 2 * block) + inside, -1)
    column = lax.broadcasted_iota(jnp.int32, (NZ * 48, W), 1)
    select = (column == source).astype(F32).astype(BF16)
    picked = lax.dot_general(
        select, rows_ref[...], (((1,), (1,)), ((), ())), preferred_element_type=F32
    )
    pick_ref[...] = picked.astype(BF16)


def fold_product(grown):
    rows = grown.shape[0]
    while rows > 8:
        rows //= 2
        one, two = grown[:rows], grown[rows:]
        grown = one + two + one * two
    return grown


def fold_sum(values):
    rows = values.shape[0]
    while rows > 8:
        rows //= 2
        values = values[:rows] + values[rows:]
    return values


def log1p(value):
    up = 1.0 + value
    gap = up - 1.0
    return jnp.where(gap == 0.0, value, jnp.log(up) * (value / jnp.where(gap == 0.0, 1.0, gap)))


def pair_terms(scale_ref, bias_ref, img_ref, texts, text, slope):
    text[: 7 * ROWS, :] = texts[0][...]
    text[7 * ROWS :, :] = texts[1][...]
    scale, bias = scale_ref[0], bias_ref[0]
    total = jnp.zeros((8, 128), F32)
    span = 2
    for start in range(0, 8, span):
        sims = lax.dot_general(
            img_ref[...],
            text[pl.ds(start * ROWS, span * ROWS), :],
            (((1,), (1,)), ((), ())),
            preferred_element_type=F32,
        )
        for half in range(span):
            chunk = start + half
            turned = scale * sims[:, half * ROWS : (half + 1) * ROWS] + bias
            if chunk == 0:
                shape = (4 * ROWS, ROWS)
                match = lax.broadcasted_iota(jnp.int32, shape, 0) == lax.broadcasted_iota(
                    jnp.int32, shape, 1
                )
                turned = jnp.where(match, -turned, turned)
            small = jnp.exp(-jnp.abs(turned))
            below = 1.0 + small
            inverse = pltpu.reciprocal(below, approx=True)
            inverse = inverse * (2.0 - below * inverse)
            sig = jnp.where(turned >= 0.0, 1.0, small) * inverse
            if chunk == 0:
                sig = jnp.where(match, -sig, sig)
            slope[:, chunk * ROWS : (chunk + 1) * ROWS] = sig.astype(BF16)
            total = total + fold_sum(jnp.maximum(turned, 0.0)) + log1p(fold_product(small))
    return total


def pairs_kernel(scale_ref, bias_ref, img_ref, *refs):
    texts, (send_ref, loss_ref, slope, text) = refs[:2], refs[2:]
    total = pair_terms(scale_ref, bias_ref, img_ref, texts, text, slope)
    loss = jnp.broadcast_to(jnp.sum(total, keepdims=True), (1, 128))
    loss_ref[...] = loss
    grad = jnp.dot(slope[2 * ROWS :, :], text[...], preferred_element_type=F32)
    send_ref[: 2 * ROWS, :] = grad.astype(BF16)
    send_ref[2 * ROWS :, :] = loss_rows(loss)


def keep_kernel(slope_ref, early_ref, last_ref, keep_ref):
    early = jnp.dot(slope_ref[: 2 * ROWS, : 7 * ROWS], early_ref[...], preferred_element_type=F32)
    last = jnp.dot(slope_ref[: 2 * ROWS, 7 * ROWS :], last_ref[...], preferred_element_type=F32)
    keep_ref[...] = early + last


def loss_rows(loss):
    high = loss.astype(BF16).astype(F32)
    row = jnp.concatenate([high, loss - high, jnp.zeros((1, E - 256), F32)], axis=1)
    return jnp.broadcast_to(row, (EXTRA, E)).astype(BF16)


def got_loss(got_ref):
    row = got_ref[2 * ROWS :, :256].astype(F32)[:1]
    return row[:, :128] + row[:, 128:]


def add_kernel(keep_ref, loss_ref, got_ref, send_ref):
    total = keep_ref[...] + got_ref[: 2 * ROWS, :].astype(F32)
    send_ref[: 2 * ROWS, :] = total.astype(BF16)
    loss = loss_ref[...] + got_loss(got_ref)
    send_ref[2 * ROWS :, :] = loss_rows(loss)


def dproj_kernel(
    scale_ref, keep_ref, loss_ref, core_ref, got_ref, unit_ref, pnorm_ref, after_ref, dproj_ref, loss_out
):
    del after_ref
    loss_out[...] = loss_ref[...] + got_loss(core_ref) + got_loss(got_ref)
    for i in range(2):
        rows, other = pl.ds(i * ROWS, ROWS), pl.ds((1 - i) * ROWS, ROWS)
        total = keep_ref[rows, :] + core_ref[rows, :].astype(F32)
        grad = scale_ref[0] * (total + got_ref[other, :].astype(F32))
        unit = unit_ref[rows, :]
        inner = jnp.sum(unit * grad, axis=1, keepdims=True)
        dproj_ref[rows, :] = ((grad - unit * inner) * pnorm_ref[rows, 0:1]).astype(BF16)


def back(dproj, w_ref):
    return lax.dot_general(dproj, w_ref[...], (((1,), (1,)), ((), ())), preferred_element_type=F32)


def features_kernel(dproj_ref, x_ref, gain_ref, rows_ref, w_ref, feat_ref, part_ref):
    d_normed = back(dproj_ref[...], w_ref)
    own = d_normed[:ROWS]
    part_ref[...] = jnp.sum(rows_ref[: 2 * ROWS, :].astype(F32) * d_normed, axis=0, keepdims=True)
    x_hat, scale = moments(x_ref[...].astype(F32))
    d_hat = own * gain_ref[...].reshape(1, W)
    feat = scale * (
        d_hat
        - jnp.mean(d_hat, axis=1, keepdims=True)
        - x_hat * jnp.mean(d_hat * x_hat, axis=1, keepdims=True)
    )
    feat_ref[...] = feat.astype(BF16)


def split_rows(first, second):
    high = [r.astype(BF16).astype(F32) for r in (first, second)]
    return high + [first - high[0], second - high[1]]


def head_kernel(own_ref, got_ref, pick_ref, rows_ref, w_ref, gain_ref, part_ref, loss_ref, out_ref):
    head = jnp.dot(pick_ref[:, : 2 * ROWS], own_ref[...], preferred_element_type=F32) + jnp.dot(
        pick_ref[:, 2 * ROWS :], got_ref[...], preferred_element_type=F32
    )
    d_normed = back(got_ref[...], w_ref)
    gain = part_ref[...] + jnp.sum(rows_ref[2 * ROWS :, :].astype(F32) * d_normed, axis=0, keepdims=True)
    gain = gain / gain_ref[...].reshape(1, W)
    rest = [gain[:, PIECE:], loss_ref[...], jnp.zeros((1, 2 * PIECE - W - 128), F32)]
    extra = split_rows(gain[:, :PIECE], jnp.concatenate(rest, axis=1))
    index = lax.broadcasted_iota(jnp.int32, (16, PIECE), 0)
    for k in range(NZ):
        block = head[48 * k : 48 * (k + 1)]
        at = BLOCK * k
        out_ref[at : at + 32, :] = block[:32, :PIECE].astype(BF16)
        tail = block[32:, :PIECE]
        for i, row in enumerate(extra):
            tail = jnp.where(index == 12 + i, row, tail)
        out_ref[at + 32 : at + 48, :] = tail.astype(BF16)
        for i in range(3):
            side = block[16 * i : 16 * (i + 1), PIECE:].astype(BF16)
            out_ref[at + 48 : at + 64, 256 * i : 256 * (i + 1)] = side
        out_ref[at + 48 : at + 64, 768:] = jnp.zeros((16, 128), BF16)


def reduce_kernel(got_ref, out_ref):
    total = got_ref[...].astype(F32).reshape(8 * NZ, 8, PIECE).sum(axis=0)
    index = lax.broadcasted_iota(jnp.int32, (8, PIECE), 0)
    split = total
    for i, row in enumerate(split_rows(total[4:5] + total[6:7], total[5:6] + total[7:8])):
        split = jnp.where(index == 4 + i, row, split)
    piece = jnp.where(lax.axis_index(Y) == 5, split, total)
    copies = jnp.broadcast_to(piece[None], (N_GROUP, 8, PIECE)).reshape(8 * N_GROUP, PIECE)
    out_ref[...] = copies.astype(BF16)


def unpack_kernel(got_ref, head_ref, gain_ref, loss_ref):
    block = got_ref[:BLOCK, :].astype(F32) + got_ref[BLOCK:, :].astype(F32)
    head_ref[:, :PIECE] = block[:SHARE]
    head_ref[0:16, PIECE:] = block[48:64, 0:256]
    head_ref[16:32, PIECE:] = block[48:64, 256:512]
    head_ref[32:SHARE, PIECE:] = block[48 : 48 + SHARE - 32, 512:768]
    rows = block[44:46] + block[46:48]
    gain_ref[...] = jnp.concatenate([rows[0], rows[1, : W - PIECE]])
    loss = rows[1:2, W - PIECE : W - PIECE + 128]
    loss_ref[0] = jnp.max(loss) * (1.0 / (N_GROUP * NZ * 4 * ROWS))


def per_device(pooled, captions, gain, w, scale, bias):
    x = pooled[0]
    across = functools.partial(lax.ppermute, axis_name=X, perm=SWAP)
    between = functools.partial(lax.ppermute, axis_name=C, perm=SWAP)
    hop = functools.partial(lax.ppermute, axis_name=(Z, C), perm=HOP)
    hop_back = functools.partial(lax.ppermute, axis_name=(Z, C), perm=HOP_BACK)

    text = call(text_kernel, out((ROWS, E), BF16), captions[0], name="text_unit")
    n0 = call(norm_kernel, out((ROWS, W), BF16), x, gain, name="normed")
    far = across(n0)
    texts = [text]
    one, two = text, text
    for step in range(4):
        one = hop(one)
        texts.append(one)
        if step < 3:
            two = hop_back(two)
            texts.append(two)

    n_own = call(join_kernel, out((2 * ROWS, W), BF16), n0, far, name="join")
    img, unit, pnorm, rows = call(
        project_kernel,
        (
            out((4 * ROWS, E), BF16),
            out((2 * ROWS, E), F32),
            out((2 * ROWS, 128), F32),
            out((4 * ROWS, W), BF16),
        ),
        n_own,
        between(n_own),
        w,
        texts[5],
        flops=2 * 4 * ROWS * W * E,
        name="project",
    )
    early = call(
        collect_kernel,
        out((7 * ROWS, E), BF16),
        *texts[:7],
        flops=4 * 4 * ROWS * 7 * ROWS * E,
        name="collect",
    )
    send, loss, slope = call(
        pairs_kernel,
        (
            out((2 * ROWS + EXTRA, E), BF16),
            out((1, 128), F32),
            out((4 * ROWS, 8 * ROWS), BF16),
        ),
        scale,
        bias,
        img,
        early,
        texts[7],
        specs=[SMEM] * 2 + [VMEM] * 3,
        scratch=[pltpu.VMEM((8 * ROWS, E), BF16)],
        flops=3 * 4 * ROWS * 8 * ROWS * E,
        name="pairs",
    )
    core = between(send)
    keep = call(
        keep_kernel,
        out((2 * ROWS, E), F32),
        slope,
        early,
        texts[7],
        flops=4 * ROWS * 8 * ROWS * E,
        name="keep",
    )
    send = call(
        add_kernel,
        out((2 * ROWS + EXTRA, E), BF16),
        keep,
        loss,
        core,
        mib=8,
        name="add_cores",
    )
    pick = call(
        pick_kernel,
        out((NZ * 48, 4 * ROWS), BF16),
        send,
        rows,
        flops=2 * 4 * ROWS * W * NZ * 48,
        mib=12,
        name="pick",
    )
    dproj, loss = call(
        dproj_kernel,
        (out((2 * ROWS, E), BF16), out((1, 128), F32)),
        scale,
        keep,
        loss,
        core,
        across(send),
        unit,
        pnorm,
        pick,
        specs=[SMEM] + [VMEM] * 7,
        mib=8,
        name="d_proj",
    )
    dproj_far = between(dproj)
    d_features, gain_part = call(
        features_kernel,
        (out((ROWS, W), BF16), out((1, W), F32)),
        dproj,
        x,
        gain,
        rows,
        w,
        flops=4 * ROWS * W * E,
        mib=16,
        name="d_features",
    )
    packed = call(
        head_kernel,
        out((NZ * BLOCK, PIECE), BF16),
        dproj,
        dproj_far,
        pick,
        rows,
        w,
        gain,
        gain_part,
        loss,
        flops=4 * ROWS * W * E + 8 * ROWS * NZ * 48 * E,
        mib=24,
        name="head",
    )
    packed = lax.all_to_all(packed, (Z, Y), 0, 0, tiled=True)
    piece = call(
        reduce_kernel,
        out((8 * N_GROUP, PIECE), BF16),
        packed,
        name="reduce",
    )
    block = lax.all_to_all(piece, (HX, Y), 0, 0, tiled=True)
    head, d_gain, loss = call(
        unpack_kernel,
        (out((SHARE, E), F32), out((W,), F32), out((1,), F32)),
        block,
        outs=(VMEM, VMEM, SMEM),
        name="unpack",
    )
    return loss.reshape(()), d_features[None], d_gain, head


def solution(mesh):
    fine = Mesh(mesh.devices.reshape(2, NZ, 2, 2, 8), (X, Z, C, HX, Y))
    rows = P((HX, Y), (X, Z, C), None)
    return jax.shard_map(
        per_device,
        mesh=fine,
        in_specs=(rows, rows, P(), P(), P(), P()),
        out_specs=(P(), rows, P(), P((X, Z, C), None)),
        check_vma=False,
    )
```

```python
import functools

import jax
import jax.numpy as jnp
from jax import lax
from jax.experimental import pallas as pl
from jax.experimental.pallas import tpu as pltpu
from jax.sharding import Mesh, PartitionSpec as P

EPSILON = 1e-06
ROWS = 128
W = 1408
E = 1152
SHARE = 44
F32 = jnp.float32
BF16 = jnp.bfloat16

X, Z, C, HX, Y = "x", "z", "c", "hx", "y"
NZ = 8
N_GROUP = 16
PIECE = 896
BLOCK = 64
EXTRA = 16

SWAP = [(0, 1), (1, 0)]
HOP = [
    (z * 2 + c, ((z + (1 if c == 0 else -1)) % NZ) * 2 + c) for z in range(NZ) for c in range(2)
]

HOP_BACK = [(there, here) for here, there in HOP]

VMEM = pl.BlockSpec(memory_space=pltpu.VMEM)
SMEM = pl.BlockSpec(memory_space=pltpu.SMEM)


def call(kernel, out_shape, *operands, specs=None, outs=None, scratch=(), flops=0, mib=48, name=None):
    leaves = jax.tree.leaves(out_shape)
    moved = sum(o.size * o.dtype.itemsize for o in (*operands, *leaves))
    return pl.pallas_call(
        kernel,
        out_shape=out_shape,
        in_specs=specs or [VMEM] * len(operands),
        out_specs=outs or jax.tree.map(lambda _: VMEM, out_shape),
        scratch_shapes=list(scratch),
        name=name,
        cost_estimate=pl.CostEstimate(flops=flops, bytes_accessed=moved, transcendentals=0),
        compiler_params=pltpu.CompilerParams(vmem_limit_bytes=mib << 20),
    )(*operands)


def out(shape, dtype):
    return jax.ShapeDtypeStruct(shape, dtype)


def moments(values):
    mean = jnp.mean(values, axis=1, keepdims=True)
    centred = values - mean
    scale = lax.rsqrt(jnp.mean(centred * centred, axis=1, keepdims=True) + EPSILON)
    return centred * scale, scale


def text_kernel(cap_ref, text_ref):
    values = cap_ref[...].astype(F32)
    scale = lax.rsqrt(jnp.sum(values * values, axis=1, keepdims=True) + EPSILON)
    text_ref[...] = (values * scale).astype(BF16)


def norm_kernel(x_ref, gain_ref, normed_ref):
    x_hat, _ = moments(x_ref[...].astype(F32))
    normed_ref[...] = (x_hat * gain_ref[...].reshape(1, W)).astype(BF16)


def join_kernel(own_ref, got_ref, after_ref, both_ref):
    del after_ref
    both_ref[:ROWS, :] = own_ref[...]
    both_ref[ROWS:, :] = got_ref[...]


def collect_kernel(*refs):
    for i, piece in enumerate(refs[:-1]):
        refs[-1][pl.ds(i * ROWS, ROWS), :] = piece[...]


def project_kernel(n_own, n_core, w_ref, after_ref, img_ref, unit_ref, pnorm_ref, rows_ref):
    del after_ref
    rows_ref[: 2 * ROWS, :] = n_own[...]
    rows_ref[2 * ROWS :, :] = n_core[...]
    proj = jnp.dot(rows_ref[...], w_ref[...], preferred_element_type=F32)
    pnorm = lax.rsqrt(jnp.sum(proj * proj, axis=1, keepdims=True) + EPSILON)
    unit = proj * pnorm
    img_ref[...] = unit.astype(BF16)
    unit_ref[...] = unit[: 2 * ROWS]
    pnorm_ref[...] = jnp.broadcast_to(pnorm[: 2 * ROWS], (2 * ROWS, 128))


def pick_kernel(after_ref, rows_ref, pick_ref):
    del after_ref
    row = lax.broadcasted_iota(jnp.int32, (NZ * 48, 1), 0)
    block = row // 48
    inside = row - block * 48
    device = lax.axis_index(X) * 16 + lax.axis_index(C)
    source = jnp.where(inside < SHARE, SHARE * (device + 2 * block) + inside, -1)
    column = lax.broadcasted_iota(jnp.int32, (NZ * 48, W), 1)
    select = (column == source).astype(F32).astype(BF16)
    picked = lax.dot_general(
        select, rows_ref[...], (((1,), (1,)), ((), ())), preferred_element_type=F32
    )
    pick_ref[...] = picked.astype(BF16)


def fold_product(grown):
    rows = grown.shape[0]
    while rows > 8:
        rows //= 2
        one, two = grown[:rows], grown[rows:]
        grown = one + two + one * two
    return grown


def fold_sum(values):
    rows = values.shape[0]
    while rows > 8:
        rows //= 2
        values = values[:rows] + values[rows:]
    return values


def log1p(value):
    up = 1.0 + value
    gap = up - 1.0
    return jnp.where(gap == 0.0, value, jnp.log(up) * (value / jnp.where(gap == 0.0, 1.0, gap)))


def pair_terms(scale_ref, bias_ref, img_ref, texts, text, slope):
    text[: 7 * ROWS, :] = texts[0][...]
    text[7 * ROWS :, :] = texts[1][...]
    scale, bias = scale_ref[0], bias_ref[0]
    total = jnp.zeros((8, 128), F32)
    span = 2
    for start in range(0, 8, span):
        sims = lax.dot_general(
            img_ref[...],
            text[pl.ds(start * ROWS, span * ROWS), :],
            (((1,), (1,)), ((), ())),
            preferred_element_type=F32,
        )
        for half in range(span):
            chunk = start + half
            turned = scale * sims[:, half * ROWS : (half + 1) * ROWS] + bias
            if chunk == 0:
                shape = (4 * ROWS, ROWS)
                match = lax.broadcasted_iota(jnp.int32, shape, 0) == lax.broadcasted_iota(
                    jnp.int32, shape, 1
                )
                turned = jnp.where(match, -turned, turned)
            small = jnp.exp(-jnp.abs(turned))
            below = 1.0 + small
            inverse = pltpu.reciprocal(below, approx=True)
            inverse = inverse * (2.0 - below * inverse)
            sig = jnp.where(turned >= 0.0, 1.0, small) * inverse
            if chunk == 0:
                sig = jnp.where(match, -sig, sig)
            slope[:, chunk * ROWS : (chunk + 1) * ROWS] = sig.astype(BF16)
            total = total + fold_sum(jnp.maximum(turned, 0.0)) + log1p(fold_product(small))
    return total


def pairs_kernel(scale_ref, bias_ref, img_ref, *refs):
    texts, (send_ref, loss_ref, slope, text) = refs[:2], refs[2:]
    total = pair_terms(scale_ref, bias_ref, img_ref, texts, text, slope)
    loss = jnp.broadcast_to(jnp.sum(total, keepdims=True), (1, 128))
    loss_ref[...] = loss
    grad = jnp.dot(slope[2 * ROWS :, :], text[...], preferred_element_type=F32)
    send_ref[: 2 * ROWS, :] = grad.astype(BF16)
    send_ref[2 * ROWS :, :] = loss_rows(loss)


def keep_kernel(slope_ref, early_ref, last_ref, keep_ref):
    early = jnp.dot(slope_ref[: 2 * ROWS, : 7 * ROWS], early_ref[...], preferred_element_type=F32)
    last = jnp.dot(slope_ref[: 2 * ROWS, 7 * ROWS :], last_ref[...], preferred_element_type=F32)
    keep_ref[...] = early + last


def loss_rows(loss):
    high = loss.astype(BF16).astype(F32)
    row = jnp.concatenate([high, loss - high, jnp.zeros((1, E - 256), F32)], axis=1)
    return jnp.broadcast_to(row, (EXTRA, E)).astype(BF16)


def got_loss(got_ref):
    row = got_ref[2 * ROWS :, :256].astype(F32)[:1]
    return row[:, :128] + row[:, 128:]


def add_kernel(keep_ref, loss_ref, got_ref, send_ref):
    total = keep_ref[...] + got_ref[: 2 * ROWS, :].astype(F32)
    send_ref[: 2 * ROWS, :] = total.astype(BF16)
    loss = loss_ref[...] + got_loss(got_ref)
    send_ref[2 * ROWS :, :] = loss_rows(loss)


def dproj_kernel(
    scale_ref, keep_ref, loss_ref, core_ref, got_ref, unit_ref, pnorm_ref, after_ref, dproj_ref, loss_out
):
    del after_ref
    loss_out[...] = loss_ref[...] + got_loss(core_ref) + got_loss(got_ref)
    for i in range(2):
        rows, other = pl.ds(i * ROWS, ROWS), pl.ds((1 - i) * ROWS, ROWS)
        total = keep_ref[rows, :] + core_ref[rows, :].astype(F32)
        grad = scale_ref[0] * (total + got_ref[other, :].astype(F32))
        unit = unit_ref[rows, :]
        inner = jnp.sum(unit * grad, axis=1, keepdims=True)
        dproj_ref[rows, :] = ((grad - unit * inner) * pnorm_ref[rows, 0:1]).astype(BF16)


def back(dproj, w_ref):
    return lax.dot_general(dproj, w_ref[...], (((1,), (1,)), ((), ())), preferred_element_type=F32)


def features_kernel(dproj_ref, x_ref, gain_ref, rows_ref, w_ref, feat_ref, part_ref):
    d_normed = back(dproj_ref[...], w_ref)
    own = d_normed[:ROWS]
    part_ref[...] = jnp.sum(rows_ref[: 2 * ROWS, :].astype(F32) * d_normed, axis=0, keepdims=True)
    x_hat, scale = moments(x_ref[...].astype(F32))
    d_hat = own * gain_ref[...].reshape(1, W)
    feat = scale * (
        d_hat
        - jnp.mean(d_hat, axis=1, keepdims=True)
        - x_hat * jnp.mean(d_hat * x_hat, axis=1, keepdims=True)
    )
    feat_ref[...] = feat.astype(BF16)


def split_rows(first, second):
    high = [r.astype(BF16).astype(F32) for r in (first, second)]
    return high + [first - high[0], second - high[1]]


def head_kernel(own_ref, got_ref, pick_ref, rows_ref, w_ref, gain_ref, part_ref, loss_ref, out_ref):
    head = jnp.dot(pick_ref[:, : 2 * ROWS], own_ref[...], preferred_element_type=F32) + jnp.dot(
        pick_ref[:, 2 * ROWS :], got_ref[...], preferred_element_type=F32
    )
    d_normed = back(got_ref[...], w_ref)
    gain = part_ref[...] + jnp.sum(rows_ref[2 * ROWS :, :].astype(F32) * d_normed, axis=0, keepdims=True)
    gain = gain / gain_ref[...].reshape(1, W)
    rest = [gain[:, PIECE:], loss_ref[...], jnp.zeros((1, 2 * PIECE - W - 128), F32)]
    extra = split_rows(gain[:, :PIECE], jnp.concatenate(rest, axis=1))
    index = lax.broadcasted_iota(jnp.int32, (16, PIECE), 0)
    for k in range(NZ):
        block = head[48 * k : 48 * (k + 1)]
        at = BLOCK * k
        out_ref[at : at + 32, :] = block[:32, :PIECE].astype(BF16)
        tail = block[32:, :PIECE]
        for i, row in enumerate(extra):
            tail = jnp.where(index == 12 + i, row, tail)
        out_ref[at + 32 : at + 48, :] = tail.astype(BF16)
        for i in range(3):
            side = block[16 * i : 16 * (i + 1), PIECE:].astype(BF16)
            out_ref[at + 48 : at + 64, 256 * i : 256 * (i + 1)] = side
        out_ref[at + 48 : at + 64, 768:] = jnp.zeros((16, 128), BF16)


def reduce_kernel(got_ref, out_ref):
    total = got_ref[...].astype(F32).reshape(8 * NZ, 8, PIECE).sum(axis=0)
    index = lax.broadcasted_iota(jnp.int32, (8, PIECE), 0)
    split = total
    for i, row in enumerate(split_rows(total[4:5] + total[6:7], total[5:6] + total[7:8])):
        split = jnp.where(index == 4 + i, row, split)
    piece = jnp.where(lax.axis_index(Y) == 5, split, total)
    copies = jnp.broadcast_to(piece[None], (N_GROUP, 8, PIECE)).reshape(8 * N_GROUP, PIECE)
    out_ref[...] = copies.astype(BF16)


def unpack_kernel(got_ref, head_ref, gain_ref, loss_ref):
    block = got_ref[:BLOCK, :].astype(F32) + got_ref[BLOCK:, :].astype(F32)
    head_ref[:, :PIECE] = block[:SHARE]
    head_ref[0:16, PIECE:] = block[48:64, 0:256]
    head_ref[16:32, PIECE:] = block[48:64, 256:512]
    head_ref[32:SHARE, PIECE:] = block[48 : 48 + SHARE - 32, 512:768]
    rows = block[44:46] + block[46:48]
    gain_ref[...] = jnp.concatenate([rows[0], rows[1, : W - PIECE]])
    loss = rows[1:2, W - PIECE : W - PIECE + 128]
    loss_ref[0] = jnp.max(loss) * (1.0 / (N_GROUP * NZ * 4 * ROWS))


def per_device(pooled, captions, gain, w, scale, bias):
    x = pooled[0]
    across = functools.partial(lax.ppermute, axis_name=X, perm=SWAP)
    between = functools.partial(lax.ppermute, axis_name=C, perm=SWAP)
    hop = functools.partial(lax.ppermute, axis_name=(Z, C), perm=HOP)
    hop_back = functools.partial(lax.ppermute, axis_name=(Z, C), perm=HOP_BACK)

    text = call(text_kernel, out((ROWS, E), BF16), captions[0], name="text_unit")
    n0 = call(norm_kernel, out((ROWS, W), BF16), x, gain, name="normed")
    far = across(n0)
    texts = [text]
    one, two = text, text
    for step in range(4):
        one = hop(one)
        texts.append(one)
        if step < 3:
            two = hop_back(two)
            texts.append(two)

    n_own = call(join_kernel, out((2 * ROWS, W), BF16), n0, far, texts[4], name="join")
    img, unit, pnorm, rows = call(
        project_kernel,
        (
            out((4 * ROWS, E), BF16),
            out((2 * ROWS, E), F32),
            out((2 * ROWS, 128), F32),
            out((4 * ROWS, W), BF16),
        ),
        n_own,
        between(n_own),
        w,
        texts[5],
        flops=2 * 4 * ROWS * W * E,
        name="project",
    )
    early = call(
        collect_kernel,
        out((7 * ROWS, E), BF16),
        *texts[:7],
        name="collect",
    )
    last = call(
        collect_kernel,
        out((ROWS, E), BF16),
        texts[7],
        flops=12 * 4 * ROWS * 8 * ROWS * E,
        name="last",
    )
    send, loss, slope = call(
        pairs_kernel,
        (
            out((2 * ROWS + EXTRA, E), BF16),
            out((1, 128), F32),
            out((4 * ROWS, 8 * ROWS), BF16),
        ),
        scale,
        bias,
        img,
        early,
        last,
        specs=[SMEM] * 2 + [VMEM] * 3,
        scratch=[pltpu.VMEM((8 * ROWS, E), BF16)],
        flops=3 * 4 * ROWS * 8 * ROWS * E,
        name="pairs",
    )
    core = between(send)
    keep = call(
        keep_kernel,
        out((2 * ROWS, E), F32),
        slope,
        early,
        last,
        flops=4 * ROWS * 8 * ROWS * E,
        name="keep",
    )
    send = call(
        add_kernel,
        out((2 * ROWS + EXTRA, E), BF16),
        keep,
        loss,
        core,
        mib=8,
        name="add_cores",
    )
    pick = call(
        pick_kernel,
        out((NZ * 48, 4 * ROWS), BF16),
        send,
        rows,
        flops=2 * 4 * ROWS * W * NZ * 48,
        mib=12,
        name="pick",
    )
    dproj, loss = call(
        dproj_kernel,
        (out((2 * ROWS, E), BF16), out((1, 128), F32)),
        scale,
        keep,
        loss,
        core,
        across(send),
        unit,
        pnorm,
        pick,
        specs=[SMEM] + [VMEM] * 7,
        mib=8,
        name="d_proj",
    )
    dproj_far = between(dproj)
    d_features, gain_part = call(
        features_kernel,
        (out((ROWS, W), BF16), out((1, W), F32)),
        dproj,
        x,
        gain,
        rows,
        w,
        flops=4 * ROWS * W * E,
        mib=16,
        name="d_features",
    )
    packed = call(
        head_kernel,
        out((NZ * BLOCK, PIECE), BF16),
        dproj,
        dproj_far,
        pick,
        rows,
        w,
        gain,
        gain_part,
        loss,
        flops=4 * ROWS * W * E + 8 * ROWS * NZ * 48 * E,
        mib=24,
        name="head",
    )
    packed = lax.all_to_all(packed, (Z, Y), 0, 0, tiled=True)
    piece = call(
        reduce_kernel,
        out((8 * N_GROUP, PIECE), BF16),
        packed,
        name="reduce",
    )
    block = lax.all_to_all(piece, (HX, Y), 0, 0, tiled=True)
    head, d_gain, loss = call(
        unpack_kernel,
        (out((SHARE, E), F32), out((W,), F32), out((1,), F32)),
        block,
        outs=(VMEM, VMEM, SMEM),
        name="unpack",
    )
    return loss.reshape(()), d_features[None], d_gain, head


def solution(mesh):
    fine = Mesh(mesh.devices.reshape(2, NZ, 2, 2, 8), (X, Z, C, HX, Y))
    rows = P((HX, Y), (X, Z, C), None)
    return jax.shard_map(
        per_device,
        mesh=fine,
        in_specs=(rows, rows, P(), P(), P(), P()),
        out_specs=(P(), rows, P(), P((X, Z, C), None)),
        check_vma=False,
    )
```
